32 devices in a mesh: groups: 2 (over x), tok: 16 (over z, y, core).
Axes of the slice: x: 2, y: 2, z: 4, core: 2. Of those that a mesh axis runs over, the one named last changes fastest.
Arguments:
- query_tokens: bfloat16 [3, 4096, 1024], P(None, ('groups', 'tok')), parts along dimension 1, may hold values from -6 to 6
- key_tokens: bfloat16 [3, 4096, 1024], P(None, ('groups', 'tok')), parts along dimension 1, may hold values from -6 to 6
- value_tokens: bfloat16 [3, 4096, 1024], P(None, ('groups', 'tok')), parts along dimension 1, may hold values from -6 to 6
- learn_rates: float32 [3, 4096, 2], P(None, ('groups', 'tok')), parts along dimension 1, may hold values from 0.0009765625 to 0.00390625
- fast_first: bfloat16 [2, 512, 512], P(None, 'tok'), may hold values from -0.25 to 0.25
- fast_third: bfloat16 [2, 512, 512], P(None, 'tok'), may hold values from -0.25 to 0.25
- fast_second: bfloat16 [2, 512, 512], P(None, 'tok'), may hold values from -0.25 to 0.25
- momentum_decay: float32 [2], replicated, may hold values from 0.3 to 0.95
Outputs:
- readout: bfloat16 [3, 4096, 1024], P(None, ('groups', 'tok')), parts along dimension 1
The draws below stay inside these ranges and needn't reach their ends.
There are 2 independent parts, one for each index of `groups`. The reference program is written for one: setup_inputs(seed, part) draws one part's arguments, and reference() takes and returns one part's arrays. A program takes and returns all parts, laid end to end along the dimension named above; an argument that names none is the same for every part. Nothing has to cross between parts.
All inputs are finite; a program needn't handle non-finite values.
Results may differ from the reference program's by a relative error of at most 0.0089.
Values may be sent and summed in bfloat16 or wider, within the bound.
No kernel may reach another device: no remote copies, remote signals or barrier semaphores. Data moves between devices by JAX's collectives and lax.ppermute only.
A program may use at most 64 MiB of HBM per device.

```python
import math
import jax
import jax.numpy as jnp
from jax import lax

HEADS = 2
HD = 512
FH = 512
NCHUNK = 3
TOK_DEV = 128
CH = 2048


def raised(array, key, source, target, parts, factor):
    owner, partner = [(jnp.arange(array.shape[axis_at]) // (array.shape[axis_at] // parts)).reshape([-1 if axis == axis_at else 1 for axis in range(array.ndim)]) for axis_at in (source, target)]
    chosen = jax.random.permutation(key, parts)[partner]
    strong = (owner == chosen) | (owner == (partner + parts // 2) % parts)
    return jnp.where(strong, factor * array, array)


def block_scale(key, dims, cuts, least, largest):
    gain = 1.0
    for dim, parts in cuts:
        steps = jax.random.uniform(jax.random.fold_in(jax.random.fold_in(key, 6), dim), (parts,), jnp.float32, least / len(cuts), largest / len(cuts))
        gain = gain * jnp.repeat(jnp.exp(steps), dims[dim] // parts).reshape((-1,) + (1,) * (len(dims) - 1 - dim))
    return gain


def centred(stream_key, extent, scale, most, cuts=(), kind=jnp.bfloat16):
    values = jax.random.normal(stream_key, extent, jnp.float32) * scale
    if len(cuts) > 0:
        values = block_scale(stream_key, extent, cuts, -0.22, 0.18) * values
    return jnp.clip(values, min=-most, max=most).astype(kind)


def bell_draw_with(key, shape, spread, reach, shards, heavy, kind=jnp.bfloat16):
    values = spread * jax.random.normal(key, shape, jnp.float32)
    if shards:
        values = values * block_scale(key, shape, shards, -0.22, 0.18)
    return jnp.clip(raised(values, jax.random.fold_in(key, 3), *heavy), -reach, reach).astype(kind)


def setup_inputs(seed: int = 0, part: int = 0) -> dict:
    seeds = jax.random.split(jax.random.key(seed), 9)
    own_keys = jax.random.split(jax.random.fold_in(seeds[8], part), 9)
    return {
        "query_tokens": centred(own_keys[0], (NCHUNK, CH, HEADS * HD), 1.0, 6.0, ((1, 16),)),
        "key_tokens": centred(own_keys[1], (NCHUNK, CH, HEADS * HD), 1.0, 6.0, ((1, 16),)),
        "value_tokens": bell_draw_with(own_keys[2], (NCHUNK, CH, HEADS * HD), 1.0, 6.0, ((1, 16),), (1, 2, 16, 2.0)),
        "learn_rates": jnp.clip(jnp.exp(math.log(0.00390625) - 1.3862944 * jax.random.uniform(own_keys[3], (NCHUNK, CH, HEADS), jnp.float32) ** block_scale(own_keys[3], (NCHUNK, CH, HEADS), ((1, 16),), -0.2, 0.2)), 0.0009765625, 0.00390625),
        "fast_first": centred(seeds[4], (HEADS, FH, HD), HD ** -0.5, 0.25, ((1, 16),)),
        "fast_third": centred(seeds[5], (HEADS, FH, HD), HD ** -0.5, 0.25, ((1, 16),)),
        "fast_second": centred(seeds[6], (HEADS, HD, FH), FH ** -0.5, 0.25, ((1, 16),)),
        "momentum_decay": jnp.clip(jax.random.uniform(seeds[7], (HEADS,), jnp.float32, 0.3, 0.95), 0.3, 0.95),
    }


def forward_parts(weights, inputs):
    first, third, second = weights
    length = inputs.shape[0]
    head_count = first.shape[0]
    shaped = inputs.reshape(length, head_count, -1).astype(jnp.float32)
    pre_gate = jnp.einsum('thd,hfd->htf', shaped, first.astype(jnp.float32))
    pre_up = jnp.einsum('thd,hfd->htf', shaped, third.astype(jnp.float32))
    hidden = (jax.nn.silu(pre_gate) * pre_up).astype(jnp.bfloat16)
    return (shaped, pre_gate, pre_up, hidden)

def apply_block(weights, inputs):
    shaped, pre_gate, pre_up, hidden = forward_parts(weights, inputs)
    result = jnp.einsum('htf,hdf->thd', hidden.astype(jnp.float32), weights[2].astype(jnp.float32))
    return result.reshape(inputs.shape[0], -1)

def apply_all(weights, inputs):
    blocks = inputs.reshape(CH // TOK_DEV, TOK_DEV, inputs.shape[1])
    result = lax.map(lambda piece: apply_block(weights, piece), blocks)
    return result.reshape(CH, inputs.shape[1])

def step_block(weights, keys, values, rates):
    shaped, pre_gate, pre_up, hidden = forward_parts(weights, keys)
    length = keys.shape[0]
    head_count = weights[0].shape[0]
    scaled = (rates[:, :, None] * values.reshape(length, head_count, -1).astype(jnp.float32)).astype(jnp.bfloat16).astype(jnp.float32)
    step_second = jnp.einsum('thd,htf->hdf', scaled, hidden.astype(jnp.float32))
    back = jnp.einsum('thd,hdf->htf', scaled, weights[2].astype(jnp.float32))
    sig_gate = jax.nn.sigmoid(pre_gate)
    d_gate = (back * pre_up * sig_gate * (1.0 + pre_gate * (1.0 - sig_gate))).astype(jnp.bfloat16).astype(jnp.float32)
    d_up = (back * pre_gate * sig_gate).astype(jnp.bfloat16).astype(jnp.float32)
    step_first = jnp.einsum('htf,thd->hfd', d_gate, shaped)
    step_third = jnp.einsum('htf,thd->hfd', d_up, shaped)
    return (step_first, step_third, step_second)

def step_all(weights, keys, values, rates):
    width = keys.shape[1]
    key_blocks = keys.reshape(CH // TOK_DEV, TOK_DEV, width)
    value_blocks = values.reshape(CH // TOK_DEV, TOK_DEV, width)
    rate_blocks = rates.reshape(CH // TOK_DEV, TOK_DEV, rates.shape[1])
    start = tuple((jnp.zeros(w.shape, jnp.float32) for w in weights))

    def advance(carry, pieces):
        terms = step_block(weights, pieces[0], pieces[1], pieces[2])
        return (tuple((c + s for c, s in zip(carry, terms))), None)
    total, unused = lax.scan(advance, start, (key_blocks, value_blocks, rate_blocks))
    return total

def renorm(old, moved):
    old_norm = jnp.sqrt(lax.optimization_barrier(jnp.sum(old * old, axis=-1, keepdims=True)) + 1e-06)
    moved_norm = jnp.sqrt(lax.optimization_barrier(jnp.sum(moved * moved, axis=-1, keepdims=True)) + 1e-06)
    return moved * old_norm / moved_norm

def reference(query_tokens, key_tokens, value_tokens, learn_rates, fast_first, fast_third, fast_second, momentum_decay):
    start_low = (fast_first, fast_third, fast_second)
    weights0 = tuple((w.astype(jnp.float32) for w in start_low))
    out_zero = apply_all(start_low, query_tokens[0])
    step0 = step_all(start_low, key_tokens[0], value_tokens[0], learn_rates[0])
    step1 = step_all(start_low, key_tokens[1], value_tokens[1], learn_rates[1])
    weights1 = tuple((renorm(w, w + m) for w, m in zip(weights0, step0)))
    low_one = tuple((w.astype(jnp.bfloat16) for w in weights1))
    out_one = apply_all(low_one, query_tokens[1])
    decay = momentum_decay[:, None, None]
    mom2 = tuple((decay * m + s for m, s in zip(step0, step1)))
    weights2 = tuple((renorm(w, w + m) for w, m in zip(weights1, mom2)))
    low_two = tuple((w.astype(jnp.bfloat16) for w in weights2))
    out_two = apply_all(low_two, query_tokens[2])
    return jnp.stack([out_zero, out_one, out_two]).astype(jnp.bfloat16)
```

```python
import jax
import jax.numpy as jnp
from jax import lax
from jax.sharding import PartitionSpec as P


def forward_parts(weights, inputs):
    first, third, second = weights
    length = inputs.shape[0]
    head_count = first.shape[0]
    shaped = inputs.reshape(length, head_count, -1)
    pre_gate = jnp.einsum("thd,hfd->htf", shaped, first, preferred_element_type=jnp.float32)
    pre_up = jnp.einsum("thd,hfd->htf", shaped, third, preferred_element_type=jnp.float32)
    hidden = (jax.nn.silu(pre_gate) * pre_up).astype(jnp.bfloat16)
    return (shaped, pre_gate, pre_up, hidden)


def apply_block(weights, inputs):
    shaped, pre_gate, pre_up, hidden = forward_parts(weights, inputs)
    result = jnp.einsum("htf,hdf->thd", hidden, weights[2], preferred_element_type=jnp.float32)
    return result.reshape(inputs.shape[0], -1).astype(jnp.bfloat16)


def partial_steps(weights, keys, values, rates):
    shaped, pre_gate, pre_up, hidden = forward_parts(weights, keys)
    length = keys.shape[0]
    head_count = weights[0].shape[0]
    scaled = (
        rates[:, :, None] * values.reshape(length, head_count, -1).astype(jnp.float32)
    ).astype(jnp.bfloat16)
    step_second = jnp.einsum("thd,htf->hdf", scaled, hidden, preferred_element_type=jnp.float32)
    back = jnp.einsum("thd,hdf->htf", scaled, weights[2], preferred_element_type=jnp.float32)
    sig_gate = jax.nn.sigmoid(pre_gate)
    d_gate = (back * pre_up * sig_gate * (1.0 + pre_gate * (1.0 - sig_gate))).astype(jnp.bfloat16)
    d_up = (back * pre_gate * sig_gate).astype(jnp.bfloat16)
    step_first = jnp.einsum("htf,thd->hfd", d_gate, shaped, preferred_element_type=jnp.float32)
    step_third = jnp.einsum("htf,thd->hfd", d_up, shaped, preferred_element_type=jnp.float32)
    return (step_first, step_third, step_second)


def renorm(old, moved):
    old_norm = jnp.sqrt(jnp.sum(old * old, axis=-1, keepdims=True) + 1e-06)
    moved_norm = jnp.sqrt(jnp.sum(moved * moved, axis=-1, keepdims=True) + 1e-06)
    return moved * old_norm / moved_norm


def shards(
    query_tokens,
    key_tokens,
    value_tokens,
    learn_rates,
    fast_first,
    fast_third,
    fast_second,
    momentum_decay,
):
    own = jnp.stack([fast_first, fast_third, fast_second])
    full_zero = lax.all_gather(own, "tok", axis=2, tiled=True)
    terms = [
        jnp.stack(partial_steps(full_zero, key_tokens[b], value_tokens[b], learn_rates[b]))
        for b in range(2)
    ]
    low = jnp.stack(terms).astype(jnp.bfloat16)
    summed = lax.psum_scatter(low, "tok", scatter_dimension=3, tiled=True)
    out_zero = apply_block(full_zero, query_tokens[0])
    step_zero = summed[0].astype(jnp.float32)
    step_one = summed[1].astype(jnp.float32)
    decay = momentum_decay[None, :, None, None]
    weights_zero = own.astype(jnp.float32)
    weights_one = renorm(weights_zero, weights_zero + step_zero)
    moment = decay * step_zero + step_one
    weights_two = renorm(weights_one, weights_one + moment)
    both = jnp.stack([weights_one, weights_two]).astype(jnp.bfloat16)
    full = lax.all_gather(both, "tok", axis=3, tiled=True)
    out_one = apply_block(full[0], query_tokens[1])
    out_two = apply_block(full[1], query_tokens[2])
    return jnp.stack([out_zero, out_one, out_two])


def solution(mesh):
    placed = (
        P(None, ("groups", "tok"), None),
        P(None, ("groups", "tok"), None),
        P(None, ("groups", "tok"), None),
        P(None, ("groups", "tok"), None),
        P(None, "tok", None),
        P(None, "tok", None),
        P(None, "tok", None),
        P(),
    )
    return jax.shard_map(
        shards,
        mesh=mesh,
        in_specs=placed,
        out_specs=P(None, ("groups", "tok"), None),
        check_vma=False,
    )
```

```python
import jax
import jax.numpy as jnp
from jax import lax
from jax.sharding import PartitionSpec as P

LOW = jnp.bfloat16
WIDE = jnp.float32


def dot(a, b, dims):
    return lax.dot_general(a, b, ((dims[:1], dims[1:]), ((), ())), preferred_element_type=WIDE)


def forward_parts(weights, inputs):
    pre_gate = dot(inputs, weights[0], (1, 1))
    pre_up = dot(inputs, weights[1], (1, 1))
    hidden = (jax.nn.silu(pre_gate) * pre_up).astype(LOW)
    return pre_gate, pre_up, hidden


def partial_readout(weights, inputs):
    hidden = forward_parts(weights, inputs)[2]
    return dot(hidden, weights[2], (1, 1))


def partial_steps(weights, keys, scaled):
    pre_gate, pre_up, hidden = forward_parts(weights, keys)
    step_second = dot(scaled, hidden, (0, 0))
    back = dot(scaled, weights[2], (1, 0))
    sig_gate = jax.nn.sigmoid(pre_gate)
    d_gate = (back * pre_up * sig_gate * (1.0 + pre_gate * (1.0 - sig_gate))).astype(LOW)
    d_up = (back * pre_gate * sig_gate).astype(LOW)
    step_first = dot(d_gate, keys, (0, 0))
    step_third = dot(d_up, keys, (0, 0))
    return step_first, step_third, step_second


def renorm(old, moved):
    def norm(parts):
        return jnp.sqrt(sum(jnp.sum(p * p, axis=-1, keepdims=True) for p in parts) + 1e-06)

    factor = norm(old), norm(moved)
    return [m * factor[0] / factor[1] for m in moved]


def shards(
    query_tokens,
    key_tokens,
    value_tokens,
    learn_rates,
    fast_first,
    fast_third,
    fast_second,
    momentum_decay,
):
    count = lax.axis_size("tok")
    planes = count // 4
    index = lax.axis_index("tok")
    z, y, c = index // 4, (index // 2) % 2, index % 2
    width = fast_first.shape[2]
    half = width // 2
    rows = 2 * fast_first.shape[1]

    def send(array, dz, dy, dc):
        pairs = []
        for t in range(count):
            tz, ty, tc = t // 4, (t // 2) % 2, t % 2
            pairs.append((t, ((tz + dz) % planes) * 4 + (ty ^ dy) * 2 + (tc ^ dc)))
        return lax.ppermute(array, "tok", pairs)

    def swapped(flag, a, b, axis):
        return jnp.where(flag == 0, jnp.concatenate([a, b], axis), jnp.concatenate([b, a], axis))

    def head(array, which):
        return lax.dynamic_slice_in_dim(array, which * width, width, array.ndim - 1)

    quad = [(0, 0), (0, 1), (1, 0), (1, 1)]

    def in_quad(array):
        pieces = [head(array, c)]
        pieces += [send(head(array, c ^ dc), 0, dy, dc) for dy, dc in quad[1:]]
        return jnp.concatenate(pieces, axis=array.ndim - 2)

    def from_quad(partial):
        tokens = partial.shape[0] // 4
        pieces = [partial[i * tokens : (i + 1) * tokens] for i in range(4)]
        got = [send(pieces[i].astype(LOW), 0, *quad[i]).astype(WIDE) for i in range(1, 4)]
        mine = (pieces[0] + got[1]).astype(LOW)
        other = (got[0] + got[2]).astype(LOW)
        return swapped(c, mine, other, 1)

    def rolled(array):
        double = jnp.concatenate([array, array], axis=0)
        return lax.dynamic_slice_in_dim(double, planes - z, planes, 0)

    def gathered(same, other):
        sames = jnp.stack([same] + [send(same, planes - s, 0, 0) for s in range(1, planes)])
        others = jnp.stack([send(other, (planes - s) % planes, 1, 0) for s in range(planes)])
        sames, others = rolled(sames), rolled(others)
        first = sames[:, :, :width].reshape(half, width)
        third = sames[:, :, width : 2 * width].reshape(half, width)
        second = swapped(y, sames[:, None, :, 2 * width :], others[:, None], 1)
        return first, third, second.reshape(width, half)

    def reduced(steps):
        first = steps[0].reshape(planes, rows, width)
        third = steps[1].reshape(planes, rows, width)
        second = steps[2].reshape(planes, 2, rows, half)

        def same_for(s):
            at = (z + s) % planes
            return jnp.concatenate([first[at], third[at], second[at, y]], axis=1)

        same = same_for(0)
        for s in range(1, planes):
            same = same + send(same_for(s).astype(LOW), s, 0, 0).astype(WIDE)
        other = 0.0
        for s in range(planes):
            piece = second[(z + s) % planes, 1 - y].astype(LOW)
            other = other + send(piece, s, 1, 0).astype(WIDE)
        return same[:, :width], same[:, width : 2 * width], same[:, 2 * width :], other

    def updated(old, step):
        moved = [o + s for o, s in zip(old, step)]
        return renorm(old[:1], moved[:1]) + renorm(old[1:2], moved[1:2]) + renorm(old[2:], moved[2:])

    def spread(weights):
        low = [w.astype(LOW) for w in weights]
        return gathered(jnp.concatenate(low[:3], axis=1), low[3])

    own = jnp.stack([fast_first, fast_third, fast_second])
    mine = lax.dynamic_index_in_dim(own, c, 1, False)
    given = send(lax.dynamic_index_in_dim(own, c ^ 1, 1, False), 0, 0, 1)
    chip = swapped(c, mine, given, 1)
    columns = chip[2].reshape(rows, planes, 2, rows)
    second_same = lax.dynamic_index_in_dim(columns, y, 2, False).reshape(rows, half)
    second_other = lax.dynamic_index_in_dim(columns, 1 - y, 2, False).reshape(rows, half)
    zero = [chip[0], chip[1], second_same, second_other]
    full_zero = spread(zero)

    tokens = key_tokens.shape[1]
    scaled = learn_rates[:2, :, :, None] * value_tokens[:2].reshape(2, tokens, 2, width).astype(WIDE)
    scaled = scaled.astype(LOW).reshape(2, tokens, 2 * width)
    terms = []
    for b in range(2):
        pair = in_quad(jnp.stack([key_tokens[b], scaled[b]]))
        terms.append(partial_steps(full_zero, pair[0], pair[1]))
    queries = in_quad(query_tokens)
    out_zero = from_quad(partial_readout(full_zero, queries[0]))

    step_zero = reduced(terms[0])
    weights_zero = [w.astype(WIDE) for w in zero]
    weights_one = updated(weights_zero, step_zero)
    full_one = spread(weights_one)
    out_one = from_quad(partial_readout(full_one, queries[1]))
    step_one = reduced(terms[1])
    decay = lax.dynamic_index_in_dim(momentum_decay, c, 0, False)
    moment = [decay * m + s for m, s in zip(step_zero, step_one)]
    weights_two = updated(weights_one, moment)
    full_two = spread(weights_two)
    out_two = from_quad(partial_readout(full_two, queries[2]))
    return jnp.stack([out_zero, out_one, out_two])


def solution(mesh):
    placed = (
        P(None, ("groups", "tok"), None),
        P(None, ("groups", "tok"), None),
        P(None, ("groups", "tok"), None),
        P(None, ("groups", "tok"), None),
        P(None, "tok", None),
        P(None, "tok", None),
        P(None, "tok", None),
        P(),
    )
    return jax.shard_map(
        shards,
        mesh=mesh,
        in_specs=placed,
        out_specs=P(None, ("groups", "tok"), None),
        check_vma=False,
    )
```

```python
import jax
import jax.numpy as jnp
from jax import lax
from jax.sharding import Mesh, PartitionSpec as P

LOW = jnp.bfloat16
WIDE = jnp.float32


def dot(a, b, dims):
    return lax.dot_general(a, b, ((dims[:1], dims[1:]), ((), ())), preferred_element_type=WIDE)


def forward_parts(weights, inputs):
    pre_gate = dot(inputs, weights[0], (1, 1))
    pre_up = dot(inputs, weights[1], (1, 1))
    hidden = (jax.nn.silu(pre_gate) * pre_up).astype(LOW)
    return pre_gate, pre_up, hidden


def partial_readout(weights, inputs):
    hidden = forward_parts(weights, inputs)[2]
    return dot(hidden, weights[2], (1, 1))


def partial_steps(weights, keys, scaled):
    pre_gate, pre_up, hidden = forward_parts(weights, keys)
    step_second = dot(scaled, hidden, (0, 0))
    back = dot(scaled, weights[2], (1, 0))
    sig_gate = jax.nn.sigmoid(pre_gate)
    d_gate = (back * pre_up * sig_gate * (1.0 + pre_gate * (1.0 - sig_gate))).astype(LOW)
    d_up = (back * pre_gate * sig_gate).astype(LOW)
    step_first = dot(d_gate, keys, (0, 0))
    step_third = dot(d_up, keys, (0, 0))
    return step_first, step_third, step_second


def renorm(old, moved):
    old_norm = jnp.sqrt(jnp.sum(old * old, axis=-1, keepdims=True) + 1e-06)
    moved_norm = jnp.sqrt(jnp.sum(moved * moved, axis=-1, keepdims=True) + 1e-06)
    return moved * old_norm / moved_norm


def shards(
    query_tokens,
    key_tokens,
    value_tokens,
    learn_rates,
    fast_first,
    fast_third,
    fast_second,
    momentum_decay,
):
    planes = lax.axis_size("plane")
    index = lax.axis_index("quad")
    y, c = index // 2, index % 2
    width = fast_first.shape[2]
    half = width // 2
    own_rows = fast_first.shape[1]
    rows = 2 * own_rows
    tokens = key_tokens.shape[1]

    def quad_swap(array):
        return lax.all_to_all(array, "quad", 0, 0, tiled=True)

    def plane_swap(array):
        return lax.all_to_all(array, "plane", 0, 0, tiled=True)

    def across(array):
        return lax.ppermute(array, "quad", [(0, 2), (1, 3), (2, 0), (3, 1)])

    def by_head(array):
        split = array.reshape(-1, tokens, 2, width).transpose(2, 0, 1, 3)
        return jnp.concatenate([split, split], axis=0)

    def joined(array):
        return array.transpose(1, 0, 2, 3).reshape(array.shape[1], 4 * tokens, width)

    def from_quad(partial):
        got = quad_swap(partial.astype(LOW).reshape(4, tokens, width)).astype(WIDE)
        return jnp.concatenate([got[0] + got[2], got[1] + got[3]], axis=1).astype(LOW)

    def pick(flag, pair):
        return jnp.where(flag == 0, pair[0], pair[1])

    def spread(payload):
        got = plane_swap(jnp.broadcast_to(payload[None], (planes,) + payload.shape))
        first = got[:, :, :width].reshape(half, width)
        third = got[:, :, width : 2 * width].reshape(half, width)
        second = got[:, :, 2 * width :].reshape(planes, rows, 2, half).transpose(0, 2, 1, 3)
        return first, third, second.reshape(width, half)

    def halves(second):
        got = across(pick(1 - y, (second[:, 0], second[:, 1])))
        kept = pick(y, (second[:, 0], second[:, 1]))
        return jnp.where(
            y == 0, jnp.concatenate([kept, got], 1), jnp.concatenate([got, kept], 1)
        )

    def reduced(steps):
        second = steps[2].reshape(planes, 2, rows, half).transpose(0, 2, 1, 3)
        sent = jnp.concatenate(
            [
                steps[0].reshape(planes, rows, width),
                steps[1].reshape(planes, rows, width),
                second.reshape(planes, rows, width),
            ],
            axis=2,
        ).astype(LOW)
        total = jnp.sum(plane_swap(sent).astype(WIDE), axis=0)
        return total[:, :width], total[:, width : 2 * width], halves(total[:, 2 * width :].reshape(rows, 2, half))

    def as_three(parts):
        return jnp.stack([p.reshape(rows, width) for p in parts])

    own = jnp.stack([fast_first, fast_third, fast_second])
    moved = jnp.concatenate([own.transpose(1, 0, 2, 3)] * 2, axis=0)
    chip = quad_swap(moved)
    chip = chip.reshape(2, 2, 3, own_rows, width).transpose(0, 2, 1, 3, 4).reshape(2, 3, rows, width)
    mine = pick(y, (chip[0], chip[1]))
    second_all = chip[:, 2].reshape(2, rows, planes, 2, rows)
    second_y = pick(y, (second_all[:, :, :, 0], second_all[:, :, :, 1])).reshape(2, rows, half)
    full_zero = spread(jnp.concatenate([mine[0], mine[1], second_y[0], second_y[1]], axis=1))
    second_own = mine[2].reshape(rows, planes, 2, rows).transpose(0, 2, 1, 3)
    weights_zero = as_three([mine[0], mine[1], second_own]).astype(WIDE)

    scaled = learn_rates[:2, :, :, None] * value_tokens[:2].reshape(2, tokens, 2, width).astype(WIDE)
    scaled = scaled.astype(LOW).reshape(2, tokens, 2 * width)
    terms = []
    for b in range(2):
        pair = joined(quad_swap(by_head(jnp.stack([key_tokens[b], scaled[b]]))))
        terms.append(partial_steps(full_zero, pair[0], pair[1]))
    queries = joined(quad_swap(by_head(query_tokens)))
    out_zero = from_quad(partial_readout(full_zero, queries[0]))

    def payload_of(weights):
        low = weights.astype(LOW)
        return jnp.concatenate([low[0], low[1], halves(low[2].reshape(rows, 2, half))], axis=1)

    step_zero = as_three(reduced(terms[0]))
    weights_one = renorm(weights_zero, weights_zero + step_zero)
    full_one = spread(payload_of(weights_one))
    out_one = from_quad(partial_readout(full_one, queries[1]))
    step_one = as_three(reduced(terms[1]))
    decay = pick(c, momentum_decay)
    weights_two = renorm(weights_one, weights_one + (decay * step_zero + step_one))
    full_two = spread(payload_of(weights_two))
    out_two = from_quad(partial_readout(full_two, queries[2]))
    return jnp.stack([out_zero, out_one, out_two])


def solution(mesh):
    groups, count = mesh.shape["groups"], mesh.shape["tok"]
    split = Mesh(mesh.devices.reshape(groups, count // 4, 4), ("groups", "plane", "quad"))
    everywhere = P(None, ("groups", "plane", "quad"), None)
    rows = P(None, ("plane", "quad"), None)
    return jax.shard_map(
        shards,
        mesh=split,
        in_specs=(everywhere,) * 4 + (rows,) * 3 + (P(),),
        out_specs=everywhere,
        check_vma=False,
    )
```

```python
import functools

import jax
import jax.numpy as jnp
from jax import lax
from jax.experimental import pallas as pl
from jax.experimental.pallas import tpu as pltpu
from jax.sharding import Mesh, PartitionSpec as P

LOW = jnp.bfloat16
WIDE = jnp.float32


def call(kernel, outs, flops, *operands):
    shapes = [jax.ShapeDtypeStruct(s, d) for s, d in outs]
    moved = sum(a.size * a.dtype.itemsize for a in operands)
    moved += sum(s.size * s.dtype.itemsize for s in shapes)
    return pl.pallas_call(
        kernel,
        out_shape=shapes,
        in_specs=[pl.BlockSpec(memory_space=pltpu.VMEM)] * len(operands),
        out_specs=[pl.BlockSpec(memory_space=pltpu.VMEM)] * len(shapes),
        compiler_params=pltpu.CompilerParams(vmem_limit_bytes=40 * 2**20),
        cost_estimate=pl.CostEstimate(flops=flops, bytes_accessed=moved, transcendentals=0),
    )(*operands)


def dot(a, b, dims):
    return lax.dot_general(a, b, ((dims[:1], dims[1:]), ((), ())), preferred_element_type=WIDE)


def loaded(full):
    planes, rows, columns = full.shape
    width = columns // 3
    half = width // 2
    first = full[:, :, :width].reshape(half, width)
    third = full[:, :, width : 2 * width].reshape(half, width)
    pieces = []
    for z in range(planes):
        for y in range(2):
            start = 2 * width + y * half
            pieces.append(full[z, :, start : start + half])
    return first, third, jnp.concatenate(pieces, axis=0)


def steps_kernel(block, full, own, near, far, cross, sent):
    planes, rows, columns = full.shape
    width = columns // 3
    half = width // 2
    first, third, second = loaded(full)
    parts = (own, near, far, cross)
    keys = jnp.concatenate([p[2 * block] for p in parts], axis=0)
    scaled = jnp.concatenate([p[2 * block + 1] for p in parts], axis=0)
    pre_gate = dot(keys, first, (1, 1))
    pre_up = dot(keys, third, (1, 1))
    back = dot(scaled, second, (1, 0))
    sig_gate = jax.nn.sigmoid(pre_gate)
    silu = pre_gate * sig_gate
    hidden = (silu * pre_up).astype(LOW)
    d_gate = (back * pre_up * sig_gate * (1.0 + pre_gate * (1.0 - sig_gate))).astype(LOW)
    d_up = (back * silu).astype(LOW)
    step_first = dot(d_gate, keys, (0, 0)).astype(LOW)
    step_third = dot(d_up, keys, (0, 0)).astype(LOW)
    step_second = dot(scaled, hidden, (0, 0)).astype(LOW)
    sent[:, :, :width] = step_first.reshape(planes, rows, width)
    sent[:, :, width : 2 * width] = step_third.reshape(planes, rows, width)
    for z in range(planes):
        for y in range(2):
            start = 2 * width + y * half
            at = (2 * z + y) * rows
            sent[z, :, start : start + half] = step_second[at : at + rows]


def readout_kernel(block, full, own, near, far, cross, kept, to_near, to_far, to_cross):
    tokens = kept.shape[0]
    first, third, second = loaded(full)
    inputs = jnp.concatenate([p[block] for p in (own, near, far, cross)], axis=0)
    pre_gate = dot(inputs, first, (1, 1))
    pre_up = dot(inputs, third, (1, 1))
    hidden = (pre_gate * jax.nn.sigmoid(pre_gate) * pre_up).astype(LOW)
    result = dot(hidden, second, (1, 1))
    kept[...] = result[:tokens]
    for i, out in enumerate((to_near, to_far, to_cross)):
        out[...] = result[(i + 1) * tokens : (i + 2) * tokens].astype(LOW)


def square_sums(array, width):
    half = width // 2
    columns = []
    for y in range(2):
        piece = array[:, 2 * width + y * half : 2 * width + (y + 1) * half]
        columns.append(jnp.sum(piece * piece, axis=1, keepdims=True))
    return columns


def moved_kernel(got, old, momentum, decay, new_momentum, moved, sums):
    planes, rows, columns = got.shape
    width = columns // 3
    total = got[0].astype(WIDE)
    for z in range(1, planes):
        total = total + got[z].astype(WIDE)
    before = old[...].astype(WIDE)
    if momentum is not None:
        total = decay[0:1, 0:1] * momentum[...] + total
    after = before + total
    if new_momentum is not None:
        new_momentum[...] = total
    moved[...] = after
    parts = square_sums(after, width) + square_sums(before, width)
    sums[...] = jnp.concatenate(parts + [jnp.zeros((rows, 124), WIDE)], axis=1)


def first_moved_kernel(got, old, new_momentum, moved, sums):
    moved_kernel(got, old, None, None, new_momentum, moved, sums)


def second_moved_kernel(got, old, momentum, decay, moved, sums):
    moved_kernel(got, old, momentum, decay, None, moved, sums)


def scaled_kernel(moved, old, own_sums, far_sums, new, payload):
    planes, rows, columns = payload.shape
    width = columns // 3
    half = width // 2
    after = moved[...]
    before = old[...].astype(WIDE)
    sums = own_sums[...] + far_sums[...]

    def factor(old_sum, moved_sum):
        return jnp.sqrt(old_sum + 1e-06), jnp.sqrt(moved_sum + 1e-06)

    pieces = []
    for m in range(2):
        a = after[:, m * width : (m + 1) * width]
        b = before[:, m * width : (m + 1) * width]
        up, down = factor(
            jnp.sum(b * b, axis=1, keepdims=True), jnp.sum(a * a, axis=1, keepdims=True)
        )
        pieces.append(a * (up / down))
    for y in range(2):
        a = after[:, 2 * width + y * half : 2 * width + (y + 1) * half]
        up, down = factor(sums[:, y + 2 : y + 3], sums[:, y : y + 1])
        pieces.append(a * (up / down))
    result = jnp.concatenate(pieces, axis=1)
    if new is not None:
        new[...] = result
    low = result.astype(LOW)
    for z in range(planes):
        payload[z] = low


def last_scaled_kernel(moved, old, own_sums, far_sums, payload):
    scaled_kernel(moved, old, own_sums, far_sums, None, payload)


def shards(
    query_tokens,
    key_tokens,
    value_tokens,
    learn_rates,
    fast_first,
    fast_third,
    fast_second,
    momentum_decay,
):
    planes = lax.axis_size("plane")
    index = lax.axis_index("quad")
    y, c = index // 2, index % 2
    width = fast_first.shape[2]
    half = width // 2
    own_rows = fast_first.shape[1]
    rows = 2 * own_rows
    tokens = key_tokens.shape[1]

    def send(array, offset):
        return lax.ppermute(array, "quad", [(q, q ^ offset) for q in range(4)])

    def plane_swap(array):
        return lax.all_to_all(array, "plane", 0, 0, tiled=True)

    def heads(array):
        low, high = array[..., :width], array[..., width:]
        return jnp.where(c == 0, low, high), jnp.where(c == 0, high, low)

    def ordered(flag, a, b, axis):
        return jnp.where(flag == 0, jnp.concatenate([a, b], axis), jnp.concatenate([b, a], axis))

    def to_quad(array):
        mine, other = heads(array)
        return mine, send(other, 1), send(mine, 2), send(other, 3)

    columns = fast_second.reshape(2, own_rows, planes, 2, rows)
    split = [columns[:, :, :, i].reshape(2, own_rows, half) for i in range(2)]
    second_same = jnp.where(y == 0, split[0], split[1])
    second_far = jnp.where(y == 0, split[1], split[0])
    same = jnp.concatenate([fast_first, fast_third, second_same], axis=2)
    same_mine, same_other = jnp.where(c == 0, same[0], same[1]), jnp.where(c == 0, same[1], same[0])
    far_mine = jnp.where(c == 0, second_far[0], second_far[1])
    far_other = jnp.where(c == 0, second_far[1], second_far[0])
    same_rows = ordered(c, same_mine, send(same_other, 1), 0)
    far_rows = ordered(c, send(far_mine, 2), send(far_other, 3), 0)
    second_rows = ordered(y, same_rows[:, 2 * width :], far_rows, 1)
    zero = jnp.concatenate([same_rows[:, : 2 * width], second_rows], axis=1)
    full_zero = plane_swap(jnp.broadcast_to(zero[None], (planes,) + zero.shape))

    scaled = learn_rates[:2, :, :, None] * value_tokens[:2].reshape(2, tokens, 2, width).astype(WIDE)
    scaled = scaled.astype(LOW).reshape(2, tokens, 2 * width)
    pairs = jnp.stack([key_tokens[0], scaled[0], key_tokens[1], scaled[1]])
    pairs, zero = lax.optimization_barrier((pairs, zero))
    pairs = to_quad(pairs)
    query_tokens, pairs = lax.optimization_barrier((query_tokens, pairs))
    queries = to_quad(query_tokens)

    layout = (planes, rows, 3 * width)
    flat = layout[1:]
    unit = 2 * 4 * tokens * width * half

    def steps(block):
        kernel = functools.partial(steps_kernel, block)
        return call(kernel, [(layout, LOW)], 6 * unit, full_zero, *pairs)[0]

    def readout(block, full):
        kernel = functools.partial(readout_kernel, block)
        piece = (tokens, width)
        outs = [(piece, WIDE), (piece, LOW), (piece, LOW), (piece, LOW)]
        kept, near, far, cross = call(kernel, outs, 3 * unit, full, *queries)
        near, far, cross = send(near, 1), send(far, 2), send(cross, 3)
        mine = (kept + far.astype(WIDE)).astype(LOW)
        other = (near.astype(WIDE) + cross.astype(WIDE)).astype(LOW)
        return ordered(c, mine, other, 1)

    got_zero = plane_swap(steps(0))
    got_one = plane_swap(steps(1))
    out_zero = readout(0, full_zero)

    sums_shape = (rows, 128)
    step_zero, moved, sums = call(
        first_moved_kernel, [(flat, WIDE), (flat, WIDE), (sums_shape, WIDE)], 0, got_zero, zero
    )
    weights_one, payload = call(
        scaled_kernel, [(flat, WIDE), (layout, LOW)], 0, moved, zero, sums, send(sums, 2)
    )
    full_one = plane_swap(payload)
    out_one = readout(1, full_one)

    decay = jnp.broadcast_to(jnp.where(c == 0, momentum_decay[0], momentum_decay[1]), (8, 128))
    moved, sums = call(
        second_moved_kernel,
        [(flat, WIDE), (sums_shape, WIDE)],
        0,
        got_one,
        weights_one,
        step_zero,
        decay,
    )
    payload = call(
        last_scaled_kernel, [(layout, LOW)], 0, moved, weights_one, sums, send(sums, 2)
    )[0]
    full_two = plane_swap(payload)
    out_two = readout(2, full_two)
    return jnp.stack([out_zero, out_one, out_two])


def solution(mesh):
    groups, count = mesh.shape["groups"], mesh.shape["tok"]
    split = Mesh(mesh.devices.reshape(groups, count // 4, 4), ("groups", "plane", "quad"))
    everywhere = P(None, ("groups", "plane", "quad"), None)
    rows = P(None, ("plane", "quad"), None)
    return jax.shard_map(
        shards,
        mesh=split,
        in_specs=(everywhere,) * 4 + (rows,) * 3 + (P(),),
        out_specs=everywhere,
        check_vma=False,
    )
```

```python
import functools

import jax
import jax.numpy as jnp
from jax import lax
from jax.experimental import pallas as pl
from jax.experimental.pallas import tpu as pltpu
from jax.sharding import Mesh, PartitionSpec as P

LOW = jnp.bfloat16
WIDE = jnp.float32


def call(kernel, outs, flops, *operands, scratch=()):
    shapes = [jax.ShapeDtypeStruct(s, d) for s, d in outs]
    moved = sum(a.size * a.dtype.itemsize for a in operands)
    moved += sum(s.size * s.dtype.itemsize for s in shapes)
    return pl.pallas_call(
        kernel,
        out_shape=shapes,
        in_specs=[
            pl.BlockSpec(memory_space=pltpu.SMEM if a.ndim == 1 else pltpu.VMEM) for a in operands
        ],
        out_specs=[pl.BlockSpec(memory_space=pltpu.VMEM)] * len(shapes),
        scratch_shapes=[pltpu.VMEM(s, d) for s, d in scratch],
        compiler_params=pltpu.CompilerParams(vmem_limit_bytes=40 * 2**20),
        cost_estimate=pl.CostEstimate(flops=flops, bytes_accessed=moved, transcendentals=0),
    )(*operands)


def dot(a, b, dims):
    return lax.dot_general(a, b, ((dims[:1], dims[1:]), ((), ())), preferred_element_type=WIDE)


def place(pieces, where, first, third, second):
    rows, columns = pieces[0].shape
    width = columns // 3
    half = width // 2
    for distance, piece in enumerate(pieces):
        z = where[0] ^ distance
        at = pl.multiple_of(z * rows, rows)
        first[pl.ds(at, rows), :] = piece[:, :width]
        third[pl.ds(at, rows), :] = piece[:, width : 2 * width]
        for y in range(2):
            start = 2 * width + y * half
            at = pl.multiple_of((2 * z + y) * rows, rows)
            second[pl.ds(at, rows), :] = piece[:, start : start + half]


def steps_kernel(planes, where, *refs):
    pieces, parts, refs = refs[:planes], refs[planes : planes + 4], refs[planes + 4 :]
    sent, (first, third, second, new_first, new_third, new_second) = refs[:planes], refs[planes:]
    rows, columns = pieces[0].shape
    width = columns // 3
    half = width // 2
    place(pieces, where, first, third, second)
    keys = jnp.concatenate([p[0] for p in parts], axis=0)
    scaled = jnp.concatenate([p[1] for p in parts], axis=0)
    pre_gate = dot(keys, first[...], (1, 1))
    pre_up = dot(keys, third[...], (1, 1))
    back = dot(scaled, second[...], (1, 0))
    sig_gate = jax.nn.sigmoid(pre_gate)
    silu = pre_gate * sig_gate
    hidden = (silu * pre_up).astype(LOW)
    d_gate = (back * pre_up * sig_gate * (1.0 + pre_gate * (1.0 - sig_gate))).astype(LOW)
    d_up = (back * silu).astype(LOW)
    new_first[...] = dot(d_gate, keys, (0, 0))
    new_third[...] = dot(d_up, keys, (0, 0))
    new_second[...] = dot(scaled, hidden, (0, 0))
    for distance, out in enumerate(sent):
        z = where[0] ^ distance
        at = pl.ds(pl.multiple_of(z * rows, rows), rows)
        out[:, :width] = new_first[at, :].astype(out.dtype)
        out[:, width : 2 * width] = new_third[at, :].astype(out.dtype)
        for y in range(2):
            start = 2 * width + y * half
            at = pl.ds(pl.multiple_of((2 * z + y) * rows, rows), rows)
            out[:, start : start + half] = new_second[at, :].astype(out.dtype)


def readout_kernel(planes, block, where, *refs):
    pieces, parts, refs = refs[:planes], refs[planes : planes + 4], refs[planes + 4 :]
    kept, to_near, to_far, to_cross, first, third, second = refs
    tokens = kept.shape[0]
    place(pieces, where, first, third, second)
    inputs = jnp.concatenate([p[block] for p in parts], axis=0)
    pre_gate = dot(inputs, first[...], (1, 1))
    pre_up = dot(inputs, third[...], (1, 1))
    hidden = (pre_gate * jax.nn.sigmoid(pre_gate) * pre_up).astype(LOW)
    result = dot(hidden, second[...], (1, 1))
    kept[...] = result[:tokens]
    for i, out in enumerate((to_near, to_far, to_cross)):
        out[...] = result[(i + 1) * tokens : (i + 2) * tokens].astype(LOW)


def square_sums(array, width):
    half = width // 2
    columns = []
    for y in range(2):
        piece = array[:, 2 * width + y * half : 2 * width + (y + 1) * half]
        columns.append(jnp.sum(piece * piece, axis=1, keepdims=True))
    return columns


def moved_kernel(got, old, momentum, decay, new_momentum, moved, sums):
    rows, columns = old.shape
    width = columns // 3
    total = got[0][...].astype(WIDE)
    for part in got[1:]:
        total = total + part[...].astype(WIDE)
    before = old[...].astype(WIDE)
    if momentum is not None:
        total = decay[0:1, 0:1] * momentum[...] + total
    after = before + total
    if new_momentum is not None:
        new_momentum[...] = total
    moved[...] = after
    parts = square_sums(after, width) + square_sums(before, width)
    sums[...] = jnp.concatenate(parts + [jnp.zeros((rows, 124), WIDE)], axis=1)


def first_moved_kernel(old, *refs):
    moved_kernel(refs[:-3], old, None, None, *refs[-3:])


def second_moved_kernel(old, momentum, decay, *refs):
    moved_kernel(refs[:-2], old, momentum, decay, None, *refs[-2:])


def scaled_kernel(moved, old, own_sums, far_sums, new, payload):
    rows, columns = payload.shape
    width = columns // 3
    half = width // 2
    after = moved[...]
    before = old[...].astype(WIDE)
    sums = own_sums[...] + far_sums[...]

    def factor(old_sum, moved_sum):
        return jnp.sqrt(old_sum + 1e-06) / jnp.sqrt(moved_sum + 1e-06)

    pieces = []
    for m in range(2):
        a = after[:, m * width : (m + 1) * width]
        b = before[:, m * width : (m + 1) * width]
        old_sum = jnp.sum(b * b, axis=1, keepdims=True)
        pieces.append(a * factor(old_sum, jnp.sum(a * a, axis=1, keepdims=True)))
    for y in range(2):
        a = after[:, 2 * width + y * half : 2 * width + (y + 1) * half]
        pieces.append(a * factor(sums[:, y + 2 : y + 3], sums[:, y : y + 1]))
    result = jnp.concatenate(pieces, axis=1)
    if new is not None:
        new[...] = result
    payload[...] = result.astype(LOW)


def last_scaled_kernel(moved, old, own_sums, far_sums, payload):
    scaled_kernel(moved, old, own_sums, far_sums, None, payload)


def shards(
    query_tokens,
    key_tokens,
    value_tokens,
    learn_rates,
    fast_first,
    fast_third,
    fast_second,
    momentum_decay,
):
    planes = lax.axis_size("plane")
    index = lax.axis_index("quad")
    y, c = index // 2, index % 2
    width = fast_first.shape[2]
    half = width // 2
    own_rows = fast_first.shape[1]
    rows = 2 * own_rows
    tokens = key_tokens.shape[1]

    def send(array, offset):
        return lax.ppermute(array, "quad", [(q, q ^ offset) for q in range(4)])

    def to_plane(array, bit):
        return lax.ppermute(array, "plane", [(z, z ^ bit) for z in range(planes)])

    def spread(own):
        pieces = {0: own}
        bit = planes // 2
        while bit:
            for distance in list(pieces):
                pieces[distance | bit] = to_plane(pieces[distance], bit)
            bit //= 2
        return [pieces[d] for d in range(planes)]

    def gathered_sum(parts):
        parts = [[p] for p in parts]
        terms = list(parts[0])
        bit = 1
        while bit < planes:
            for distance in range(planes - bit, 0, -2 * bit):
                total = parts[distance][0]
                if len(parts[distance]) > 1:
                    total = sum(p.astype(WIDE) for p in parts[distance]).astype(LOW)
                came = to_plane(total, bit)
                parts[distance ^ bit].append(came)
                if distance == bit:
                    terms.append(came)
            bit *= 2
        return terms

    def heads(array):
        low, high = array[..., :width], array[..., width:]
        return jnp.where(c == 0, low, high), jnp.where(c == 0, high, low)

    def ordered(flag, a, b, axis):
        return jnp.where(flag == 0, jnp.concatenate([a, b], axis), jnp.concatenate([b, a], axis))

    def to_quad(array):
        mine, other = heads(array)
        return mine, send(other, 1), send(mine, 2), send(other, 3)

    columns = fast_second.reshape(2, own_rows, planes, 2, rows)
    split = [columns[:, :, :, i].reshape(2, own_rows, half) for i in range(2)]
    second_same = jnp.where(y == 0, split[0], split[1])
    second_far = jnp.where(y == 0, split[1], split[0])
    same = jnp.concatenate([fast_first, fast_third, second_same], axis=2)
    same_mine, same_other = jnp.where(c == 0, same[0], same[1]), jnp.where(c == 0, same[1], same[0])
    far_mine = jnp.where(c == 0, second_far[0], second_far[1])
    far_other = jnp.where(c == 0, second_far[1], second_far[0])
    same_rows = ordered(c, same_mine, send(same_other, 1), 0)
    far_rows = ordered(c, send(far_mine, 2), send(far_other, 3), 0)
    second_rows = ordered(y, same_rows[:, 2 * width :], far_rows, 1)
    zero = jnp.concatenate([same_rows[:, : 2 * width], second_rows], axis=1)
    full_zero = spread(zero)

    scaled = learn_rates[:2, :, :, None] * value_tokens[:2].reshape(2, tokens, 2, width).astype(WIDE)
    scaled = scaled.astype(LOW).reshape(2, tokens, 2 * width)
    pairs = [jnp.stack([key_tokens[b], scaled[b]]) for b in range(2)]
    first_pair, zero = lax.optimization_barrier((pairs[0], zero))
    pairs[0] = to_quad(first_pair)
    second_pair, pairs[0] = lax.optimization_barrier((pairs[1], pairs[0]))
    pairs[1] = to_quad(second_pair)
    query_tokens, pairs[1] = lax.optimization_barrier((query_tokens, pairs[1]))
    queries = to_quad(query_tokens)

    flat = (rows, 3 * width)
    unit = 2 * 4 * tokens * width * half
    where = lax.axis_index("plane").astype(jnp.int32).reshape(1)
    held = [((half, width), LOW), ((half, width), LOW), ((width, half), LOW)]

    def steps(block):
        kernel = functools.partial(steps_kernel, planes)
        outs = [(flat, WIDE if d % 2 == 0 else LOW) for d in range(planes)]
        made = [(s, WIDE) for s, _ in held]
        return call(
            kernel, outs, 6 * unit, where, *full_zero, *pairs[block], scratch=held + made
        )

    def readout(block, full):
        kernel = functools.partial(readout_kernel, planes, block)
        piece = (tokens, width)
        outs = [(piece, WIDE), (piece, LOW), (piece, LOW), (piece, LOW)]
        kept, near, far, cross = call(
            kernel, outs, 3 * unit, where, *full, *queries, scratch=held
        )
        near, far, cross = send(near, 1), send(far, 2), send(cross, 3)
        mine = (kept + far.astype(WIDE)).astype(LOW)
        other = (near.astype(WIDE) + cross.astype(WIDE)).astype(LOW)
        return ordered(c, mine, other, 1)

    got_zero = gathered_sum(steps(0))
    got_one = gathered_sum(steps(1))
    out_zero = readout(0, full_zero)

    sums_shape = (rows, 128)
    step_zero, moved, sums = call(
        first_moved_kernel, [(flat, WIDE), (flat, WIDE), (sums_shape, WIDE)], 0, zero, *got_zero
    )
    weights_one, payload = call(
        scaled_kernel, [(flat, WIDE), (flat, LOW)], 0, moved, zero, sums, send(sums, 2)
    )
    full_one = spread(payload)

    got_one, queries = lax.optimization_barrier((got_one, queries))
    decay = jnp.broadcast_to(jnp.where(c == 0, momentum_decay[0], momentum_decay[1]), (8, 128))
    moved, sums = call(
        second_moved_kernel,
        [(flat, WIDE), (sums_shape, WIDE)],
        0,
        weights_one,
        step_zero,
        decay,
        *got_one,
    )
    payload = call(last_scaled_kernel, [(flat, LOW)], 0, moved, weights_one, sums, send(sums, 2))[0]
    full_two = spread(payload)
    out_one = readout(1, full_one)
    out_two = readout(2, full_two)
    return jnp.stack([out_zero, out_one, out_two])


def solution(mesh):
    groups, count = mesh.shape["groups"], mesh.shape["tok"]
    split = Mesh(mesh.devices.reshape(groups, count // 4, 4), ("groups", "plane", "quad"))
    everywhere = P(None, ("groups", "plane", "quad"), None)
    rows = P(None, ("plane", "quad"), None)
    return jax.shard_map(
        shards,
        mesh=split,
        in_specs=(everywhere,) * 4 + (rows,) * 3 + (P(),),
        out_specs=everywhere,
        check_vma=False,
    )
```

```python
import functools

import jax
import jax.numpy as jnp
from jax import lax
from jax.experimental import pallas as pl
from jax.experimental.pallas import tpu as pltpu
from jax.sharding import Mesh, PartitionSpec as P

LOW = jnp.bfloat16
WIDE = jnp.float32


def call(kernel, outs, flops, *operands, scratch=()):
    shapes = [jax.ShapeDtypeStruct(s, d) for s, d in outs]
    return pl.pallas_call(
        kernel,
        out_shape=shapes,
        in_specs=[
            pl.BlockSpec(memory_space=pltpu.SMEM if a.ndim == 1 else pltpu.VMEM) for a in operands
        ],
        out_specs=[pl.BlockSpec(memory_space=pltpu.VMEM)] * len(shapes),
        scratch_shapes=[pltpu.VMEM(s, d) for s, d in scratch],
        compiler_params=pltpu.CompilerParams(vmem_limit_bytes=40 * 2**20),
        cost_estimate=pl.CostEstimate(flops=flops, bytes_accessed=1024, transcendentals=0),
    )(*operands)


def dot(a, b, dims):
    return lax.dot_general(a, b, ((dims[:1], dims[1:]), ((), ())), preferred_element_type=WIDE)


def place(pieces, where, first, third, second):
    rows, columns = pieces[0].shape
    width = columns // 3
    half = width // 2
    for distance, piece in enumerate(pieces):
        z = where[0] ^ distance
        at = pl.multiple_of(z * rows, rows)
        first[pl.ds(at, rows), :] = piece[:, :width]
        third[pl.ds(at, rows), :] = piece[:, width : 2 * width]
        for y in range(2):
            start = 2 * width + y * half
            at = pl.multiple_of((2 * z + y) * rows, rows)
            second[pl.ds(at, rows), :] = piece[:, start : start + half]


def steps_kernel(planes, where, *refs):
    pieces, parts, refs = refs[:planes], refs[planes : planes + 4], refs[planes + 4 :]
    sent, (first, third, second, new_first, new_third, new_second) = refs[:planes], refs[planes:]
    rows, columns = pieces[0].shape
    width = columns // 3
    half = width // 2
    place(pieces, where, first, third, second)
    keys = jnp.concatenate([p[0] for p in parts], axis=0)
    scaled = jnp.concatenate([p[1] for p in parts], axis=0)
    pre_gate = dot(keys, first[...], (1, 1))
    pre_up = dot(keys, third[...], (1, 1))
    back = dot(scaled, second[...], (1, 0))
    sig_gate = jax.nn.sigmoid(pre_gate)
    silu = pre_gate * sig_gate
    hidden = (silu * pre_up).astype(LOW)
    d_gate = (back * pre_up * sig_gate * (1.0 + pre_gate * (1.0 - sig_gate))).astype(LOW)
    d_up = (back * silu).astype(LOW)
    new_first[...] = dot(d_gate, keys, (0, 0))
    new_third[...] = dot(d_up, keys, (0, 0))
    new_second[...] = dot(scaled, hidden, (0, 0))
    for distance, out in enumerate(sent):
        z = where[0] ^ distance
        at = pl.ds(pl.multiple_of(z * rows, rows), rows)
        out[:, :width] = new_first[at, :].astype(out.dtype)
        out[:, width : 2 * width] = new_third[at, :].astype(out.dtype)
        for y in range(2):
            start = 2 * width + y * half
            at = pl.ds(pl.multiple_of((2 * z + y) * rows, rows), rows)
            out[:, start : start + half] = new_second[at, :].astype(out.dtype)


def readout_kernel(planes, block, where, *refs):
    pieces, parts, refs = refs[:planes], refs[planes : planes + 4], refs[planes + 4 :]
    kept, sent, first, third, second = refs
    tokens = kept.shape[0] // 2
    place(pieces, where, first, third, second)
    inputs = jnp.concatenate([p[block] for p in parts], axis=0)
    pre_gate = dot(inputs, first[...], (1, 1))
    pre_up = dot(inputs, third[...], (1, 1))
    hidden = (pre_gate * jax.nn.sigmoid(pre_gate) * pre_up).astype(LOW)
    result = dot(hidden, second[...], (1, 1))
    kept[...] = result[: 2 * tokens]
    sent[...] = result[2 * tokens :].astype(LOW)


def square_sums(array, width):
    half = width // 2
    columns = []
    for y in range(2):
        piece = array[:, 2 * width + y * half : 2 * width + (y + 1) * half]
        columns.append(jnp.sum(piece * piece, axis=1, keepdims=True))
    return columns


def moved_kernel(got, old, momentum, decay, new_momentum, moved, sums):
    rows, columns = old.shape
    width = columns // 3
    total = got[0][...].astype(WIDE)
    for part in got[1:]:
        total = total + part[...].astype(WIDE)
    before = old[...].astype(WIDE)
    if momentum is not None:
        total = decay[0:1, 0:1] * momentum[...] + total
    after = before + total
    if new_momentum is not None:
        new_momentum[...] = total
    moved[...] = after
    parts = square_sums(after, width) + square_sums(before, width)
    sums[...] = jnp.concatenate(parts + [jnp.zeros((rows, 124), WIDE)], axis=1)


def first_moved_kernel(old, *refs):
    moved_kernel(refs[:-3], old, None, None, *refs[-3:])


def second_moved_kernel(old, momentum, decay, *refs):
    moved_kernel(refs[:-2], old, momentum, decay, None, *refs[-2:])


def scaled_kernel(moved, old, own_sums, far_sums, new, payload):
    rows, columns = payload.shape
    width = columns // 3
    half = width // 2
    after = moved[...]
    before = old[...].astype(WIDE)
    sums = own_sums[...] + far_sums[...]

    def factor(old_sum, moved_sum):
        return jnp.sqrt(old_sum + 1e-06) / jnp.sqrt(moved_sum + 1e-06)

    pieces = []
    for m in range(2):
        a = after[:, m * width : (m + 1) * width]
        b = before[:, m * width : (m + 1) * width]
        old_sum = jnp.sum(b * b, axis=1, keepdims=True)
        pieces.append(a * factor(old_sum, jnp.sum(a * a, axis=1, keepdims=True)))
    for y in range(2):
        a = after[:, 2 * width + y * half : 2 * width + (y + 1) * half]
        pieces.append(a * factor(sums[:, y + 2 : y + 3], sums[:, y : y + 1]))
    result = jnp.concatenate(pieces, axis=1)
    if new is not None:
        new[...] = result
    payload[...] = result.astype(LOW)


def last_scaled_kernel(moved, old, own_sums, far_sums, payload):
    scaled_kernel(moved, old, own_sums, far_sums, None, payload)


def shards(
    query_tokens,
    key_tokens,
    value_tokens,
    learn_rates,
    fast_first,
    fast_third,
    fast_second,
    momentum_decay,
):
    planes = lax.axis_size("plane")
    index = lax.axis_index("quad")
    y, c = index // 2, index % 2
    width = fast_first.shape[2]
    half = width // 2
    own_rows = fast_first.shape[1]
    rows = 2 * own_rows
    tokens = key_tokens.shape[1]

    def send(array, offset):
        return lax.ppermute(array, "quad", [(q, q ^ offset) for q in range(4)])

    def to_plane(array, bit):
        return lax.ppermute(array, "plane", [(z, z ^ bit) for z in range(planes)])

    def spread(own):
        pieces = {0: own}
        bit = planes // 2
        while bit:
            for distance in list(pieces):
                pieces[distance | bit] = to_plane(pieces[distance], bit)
            bit //= 2
        return [pieces[d] for d in range(planes)]

    def halve(parts, bit):
        for distance in range(planes - bit, 0, -2 * bit):
            total = parts[distance][0]
            if len(parts[distance]) > 1:
                total = sum(p.astype(WIDE) for p in parts[distance]).astype(LOW)
            parts[distance ^ bit].append(to_plane(total, bit))

    def pick(flag, a, b):
        return jnp.where(flag == 0, a, b), jnp.where(flag == 0, b, a)

    def ordered(flag, a, b, axis):
        return jnp.where(flag == 0, jnp.concatenate([a, b], axis), jnp.concatenate([b, a], axis))

    def to_quad(array):
        mine, other = pick(y, array[..., :width], array[..., width:])
        far = send(other, 2)
        return mine, far, send(mine, 1), send(far, 1)

    columns = fast_second.reshape(2, own_rows, 2 * planes, 2, own_rows)
    split = [columns[:, :, :, i].reshape(2, own_rows, half) for i in range(2)]
    second_same, second_other = pick(c, split[0], split[1])
    same = jnp.concatenate([fast_first, fast_third, second_same], axis=2)
    same_mine, same_far = pick(y, same[0], same[1])
    near_mine, near_far = pick(y, second_other[0], second_other[1])
    same_far = send(same_far, 2)
    near_mine, near_far = send(near_mine, 1), send(near_far, 3)
    layers = ordered(y, same_mine[:, : 2 * width], same_far[:, : 2 * width], 0)
    second_mine = ordered(c, same_mine[:, 2 * width :], near_mine, 0)
    second_far = ordered(c, same_far[:, 2 * width :], near_far, 0)
    zero = jnp.concatenate([layers, ordered(y, second_mine, second_far, 1)], axis=1)
    full_zero = spread(zero)

    scaled = learn_rates[:2, :, :, None] * value_tokens[:2].reshape(2, tokens, 2, width).astype(WIDE)
    scaled = scaled.astype(LOW).reshape(2, tokens, 2 * width)
    pairs = [jnp.stack([key_tokens[b], scaled[b]]) for b in range(2)]
    pairs[0] = to_quad(pairs[0])
    second_pair, pairs[0] = lax.optimization_barrier((pairs[1], pairs[0]))
    pairs[1] = to_quad(second_pair)
    query_tokens, pairs[1] = lax.optimization_barrier((query_tokens, pairs[1]))
    queries = to_quad(query_tokens)

    flat = (rows, 3 * width)
    unit = 2 * 4 * tokens * width * half
    where = lax.axis_index("plane").astype(jnp.int32).reshape(1)
    held = [((half, width), LOW), ((half, width), LOW), ((width, half), LOW)]

    def steps(block):
        kernel = functools.partial(steps_kernel, planes)
        outs = [(flat, WIDE if d % 2 == 0 else LOW) for d in range(planes)]
        made = [(s, WIDE) for s, _ in held]
        made = call(kernel, outs, 6 * unit, where, *full_zero, *pairs[block], scratch=held + made)
        return [[part] for part in made]

    def readout(block, full):
        kernel = functools.partial(readout_kernel, planes, block)
        outs = [((2 * tokens, width), WIDE), ((2 * tokens, width), LOW)]
        kept, sent = call(kernel, outs, 3 * unit, where, *full, *queries, scratch=held)
        total = (kept + send(sent, 1).astype(WIDE)).astype(LOW)
        return ordered(y, total[:tokens], send(total[tokens:], 2), 1)

    parts = [steps(0), steps(1)]
    bit = 1
    while bit < planes:
        halve(parts[0], bit)
        later = slice(2 * bit, None, 2 * bit)
        if parts[0][later]:
            parts[0][later], parts[1][bit :: 2 * bit] = lax.optimization_barrier(
                (parts[0][later], parts[1][bit :: 2 * bit])
            )
        halve(parts[1], bit)
        bit *= 2
    got_zero, got_one = parts[0][0], parts[1][0]
    out_zero = readout(0, full_zero)

    sums_shape = (rows, 128)
    step_zero, moved, sums = call(
        first_moved_kernel, [(flat, WIDE), (flat, WIDE), (sums_shape, WIDE)], 0, zero, *got_zero
    )
    weights_one, payload = call(
        scaled_kernel, [(flat, WIDE), (flat, LOW)], 0, moved, zero, sums, send(sums, 1)
    )
    full_one = spread(payload)

    got_one, out_zero = lax.optimization_barrier((got_one, out_zero))
    decay = jnp.broadcast_to(jnp.where(y == 0, momentum_decay[0], momentum_decay[1]), (8, 128))
    moved, sums = call(
        second_moved_kernel,
        [(flat, WIDE), (sums_shape, WIDE)],
        0,
        weights_one,
        step_zero,
        decay,
        *got_one,
    )
    payload = call(last_scaled_kernel, [(flat, LOW)], 0, moved, weights_one, sums, send(sums, 1))[0]
    full_two = spread(payload)
    out_one = readout(1, full_one)
    out_two = readout(2, full_two)
    return jnp.stack([out_zero, out_one, out_two])


def solution(mesh):
    groups, count = mesh.shape["groups"], mesh.shape["tok"]
    split = Mesh(mesh.devices.reshape(groups, count // 4, 4), ("groups", "plane", "quad"))
    everywhere = P(None, ("groups", "plane", "quad"), None)
    rows = P(None, ("plane", "quad"), None)
    return jax.shard_map(
        shards,
        mesh=split,
        in_specs=(everywhere,) * 4 + (rows,) * 3 + (P(),),
        out_specs=everywhere,
        check_vma=False,
    )
```

```python
import functools

import jax
import jax.numpy as jnp
from jax import lax
from jax.experimental import pallas as pl
from jax.experimental.pallas import tpu as pltpu
from jax.sharding import Mesh, PartitionSpec as P

LOW = jnp.bfloat16
WIDE = jnp.float32


def call(kernel, outs, flops, *operands, scratch=(), behind=()):
    inner, used = kernel, len(operands)

    def kernel(*refs):
        inner(*refs[:used], *refs[used + len(behind) :])

    shapes = [jax.ShapeDtypeStruct(s, d) for s, d in outs]
    return pl.pallas_call(
        kernel,
        out_shape=shapes,
        in_specs=[
            pl.BlockSpec(memory_space=pltpu.SMEM if a.ndim == 1 else pltpu.VMEM) for a in operands
        ]
        + [pl.BlockSpec(memory_space=pl.ANY)] * len(behind),
        out_specs=[pl.BlockSpec(memory_space=pltpu.VMEM)] * len(shapes),
        scratch_shapes=[pltpu.VMEM(s, d) for s, d in scratch],
        compiler_params=pltpu.CompilerParams(vmem_limit_bytes=20 * 2**20),
        cost_estimate=pl.CostEstimate(flops=flops, bytes_accessed=1024, transcendentals=0),
    )(*operands, *behind)


def after(value, others, sink):
    value, others = lax.optimization_barrier((value, list(others)))
    sink.extend(others)
    return value


def dot(a, b, dims):
    return lax.dot_general(a, b, ((dims[:1], dims[1:]), ((), ())), preferred_element_type=WIDE)


def place(pieces, where, first, third, second):
    rows, columns = pieces[0].shape
    width = columns // 3
    half = width // 2
    for distance, piece in enumerate(pieces):
        z = where[0] ^ distance
        at = pl.multiple_of(z * rows, rows)
        first[pl.ds(at, rows), :] = piece[:, :width]
        third[pl.ds(at, rows), :] = piece[:, width : 2 * width]
        for y in range(2):
            start = 2 * width + y * half
            at = pl.multiple_of((2 * z + y) * rows, rows)
            second[pl.ds(at, rows), :] = piece[:, start : start + half]


def steps_kernel(planes, where, *refs):
    pieces, parts, refs = refs[:planes], refs[planes : planes + 4], refs[planes + 4 :]
    sent, (first, third, second, new_first, new_third, new_second) = refs[:planes], refs[planes:]
    rows, columns = pieces[0].shape
    width = columns // 3
    half = width // 2
    place(pieces, where, first, third, second)
    keys = jnp.concatenate([p[0] for p in parts], axis=0)
    scaled = jnp.concatenate([p[1] for p in parts], axis=0)
    pre_gate = dot(keys, first[...], (1, 1))
    pre_up = dot(keys, third[...], (1, 1))
    back = dot(scaled, second[...], (1, 0))
    sig_gate = jax.nn.sigmoid(pre_gate)
    silu = pre_gate * sig_gate
    hidden = (silu * pre_up).astype(LOW)
    d_gate = (back * pre_up * sig_gate * (1.0 + pre_gate * (1.0 - sig_gate))).astype(LOW)
    d_up = (back * silu).astype(LOW)
    new_first[...] = dot(d_gate, keys, (0, 0))
    new_third[...] = dot(d_up, keys, (0, 0))
    new_second[...] = dot(scaled, hidden, (0, 0))
    for distance, out in enumerate(sent):
        z = where[0] ^ distance
        at = pl.ds(pl.multiple_of(z * rows, rows), rows)
        out[:, :width] = new_first[at, :].astype(out.dtype)
        out[:, width : 2 * width] = new_third[at, :].astype(out.dtype)
        for y in range(2):
            start = 2 * width + y * half
            at = pl.ds(pl.multiple_of((2 * z + y) * rows, rows), rows)
            out[:, start : start + half] = new_second[at, :].astype(out.dtype)


def readout_kernel(planes, block, where, *refs):
    pieces, parts, refs = refs[:planes], refs[planes : planes + 4], refs[planes + 4 :]
    kept, sent, first, third, second = refs
    tokens = kept.shape[0] // 2
    place(pieces, where, first, third, second)
    inputs = jnp.concatenate([p[block] for p in parts], axis=0)
    pre_gate = dot(inputs, first[...], (1, 1))
    pre_up = dot(inputs, third[...], (1, 1))
    hidden = (pre_gate * jax.nn.sigmoid(pre_gate) * pre_up).astype(LOW)
    result = dot(hidden, second[...], (1, 1))
    kept[...] = result[: 2 * tokens]
    sent[...] = result[2 * tokens :].astype(LOW)


def square_sums(array, width):
    half = width // 2
    columns = []
    for y in range(2):
        piece = array[:, 2 * width + y * half : 2 * width + (y + 1) * half]
        columns.append(jnp.sum(piece * piece, axis=1, keepdims=True))
    return columns


def moved_kernel(got, old, momentum, decay, new_momentum, moved, sums):
    rows, columns = old.shape
    width = columns // 3
    total = got[0][...].astype(WIDE)
    for part in got[1:]:
        total = total + part[...].astype(WIDE)
    before = old[...].astype(WIDE)
    if momentum is not None:
        total = decay[0:1, 0:1] * momentum[...] + total
    after = before + total
    if new_momentum is not None:
        new_momentum[...] = total
    moved[...] = after
    parts = square_sums(after, width) + square_sums(before, width)
    sums[...] = jnp.concatenate(parts + [jnp.zeros((rows, 124), WIDE)], axis=1)


def first_moved_kernel(old, *refs):
    moved_kernel(refs[:-3], old, None, None, *refs[-3:])


def second_moved_kernel(old, momentum, decay, *refs):
    moved_kernel(refs[:-2], old, momentum, decay, None, *refs[-2:])


def scaled_kernel(moved, old, own_sums, far_sums, new, payload):
    rows, columns = payload.shape
    width = columns // 3
    half = width // 2
    after = moved[...]
    before = old[...].astype(WIDE)
    sums = own_sums[...] + far_sums[...]

    def factor(old_sum, moved_sum):
        return jnp.sqrt(old_sum + 1e-06) / jnp.sqrt(moved_sum + 1e-06)

    pieces = []
    for m in range(2):
        a = after[:, m * width : (m + 1) * width]
        b = before[:, m * width : (m + 1) * width]
        old_sum = jnp.sum(b * b, axis=1, keepdims=True)
        pieces.append(a * factor(old_sum, jnp.sum(a * a, axis=1, keepdims=True)))
    for y in range(2):
        a = after[:, 2 * width + y * half : 2 * width + (y + 1) * half]
        pieces.append(a * factor(sums[:, y + 2 : y + 3], sums[:, y : y + 1]))
    result = jnp.concatenate(pieces, axis=1)
    if new is not None:
        new[...] = result
    payload[...] = result.astype(LOW)


def last_scaled_kernel(moved, old, own_sums, far_sums, payload):
    scaled_kernel(moved, old, own_sums, far_sums, None, payload)


def shards(
    query_tokens,
    key_tokens,
    value_tokens,
    learn_rates,
    fast_first,
    fast_third,
    fast_second,
    momentum_decay,
):
    planes = lax.axis_size("plane")
    index = lax.axis_index("quad")
    y, c = index // 2, index % 2
    width = fast_first.shape[2]
    half = width // 2
    own_rows = fast_first.shape[1]
    rows = 2 * own_rows
    tokens = key_tokens.shape[1]

    def send(array, offset):
        return lax.ppermute(array, "quad", [(q, q ^ offset) for q in range(4)])

    def to_plane(array, bit):
        return lax.ppermute(array, "plane", [(z, z ^ bit) for z in range(planes)])

    def spread(own):
        return {0: own, planes // 2: to_plane(own, planes // 2)}

    def spread_on(pieces, gate=None, sink=None):
        bit = planes // 4
        while bit:
            for distance in list(pieces):
                piece = pieces[distance]
                if distance and gate is not None:
                    piece = after(piece, gate, sink)
                pieces[distance | bit] = to_plane(piece, bit)
            bit //= 2
        return [pieces[d] for d in range(planes)]

    def totals(parts, bit):
        return {
            d: sum(p.astype(WIDE) for p in parts[d]).astype(LOW)
            for d in range(planes - bit, 0, -2 * bit)
        }

    def halve(parts, bit, sent):
        for distance, total in sent.items():
            parts[distance ^ bit].append(to_plane(total, bit))

    def pick(flag, a, b):
        return jnp.where(flag == 0, a, b), jnp.where(flag == 0, b, a)

    def ordered(flag, a, b, axis):
        return jnp.where(flag == 0, jnp.concatenate([a, b], axis), jnp.concatenate([b, a], axis))

    def to_quad(array, gate=None, sink=None):
        mine, other = pick(y, array[..., :width], array[..., width:])
        far = send(other, 2)
        passed = far if gate is None else after(far, gate, sink)
        return mine, far, send(mine, 1), send(passed, 1)

    columns = fast_second.reshape(2, own_rows, 2 * planes, 2, own_rows)
    split = [columns[:, :, :, i].reshape(2, own_rows, half) for i in range(2)]
    second_same, second_other = pick(c, split[0], split[1])
    same = jnp.concatenate([fast_first, fast_third, second_same], axis=2)
    same_mine, same_far = pick(y, same[0], same[1])
    near_mine, near_far = pick(y, second_other[0], second_other[1])
    same_far = send(same_far, 2)
    near_mine, near_far = send(near_mine, 1), send(near_far, 3)
    layers = ordered(y, same_mine[:, : 2 * width], same_far[:, : 2 * width], 0)
    second_mine = ordered(c, same_mine[:, 2 * width :], near_mine, 0)
    second_far = ordered(c, same_far[:, 2 * width :], near_far, 0)
    zero = jnp.concatenate([layers, ordered(y, second_mine, second_far, 1)], axis=1)
    full_zero = spread_on(spread(zero))

    scaled = learn_rates[:2, :, :, None] * value_tokens[:2].reshape(2, tokens, 2, width).astype(WIDE)
    scaled = scaled.astype(LOW).reshape(2, tokens, 2 * width)
    pairs = [jnp.stack([key_tokens[b], scaled[b]]) for b in range(2)]
    flat = (rows, 3 * width)
    unit = 2 * 4 * tokens * width * half
    where = lax.axis_index("plane").astype(jnp.int32).reshape(1)
    held = [((half, width), LOW), ((half, width), LOW), ((width, half), LOW)]

    behind = {name: [] for name in ("steps0", "steps1", "out0", "new0", "new1", "out1", "out2")}

    def steps(block):
        kernel = functools.partial(steps_kernel, planes)
        outs = [(flat, WIDE if d % 2 == 0 else LOW) for d in range(planes)]
        made = [(s, WIDE) for s, _ in held]
        made = call(
            kernel,
            outs,
            6 * unit,
            where,
            *full_zero,
            *pairs[block],
            scratch=held + made,
            behind=behind["steps%d" % block],
        )
        return [[part] for part in made]

    def readout(block, full):
        kernel = functools.partial(readout_kernel, planes, block)
        outs = [((2 * tokens, width), WIDE), ((2 * tokens, width), LOW)]
        kept, sent = call(
            kernel,
            outs,
            3 * unit,
            where,
            *full,
            *queries,
            scratch=held,
            behind=behind["out%d" % block],
        )
        return (kept + send(sent, 1).astype(WIDE)).astype(LOW)

    def returned(total):
        return ordered(y, total[:tokens], send(total[tokens:], 2), 1)

    pairs[0] = to_quad(
        after(pairs[0], [full_zero[planes // 2]], behind["steps0"]),
        [full_zero[1], full_zero[planes - 1]],
        behind["steps0"],
    )
    zeros = steps(0)
    halve(zeros, 1, totals(zeros, 1))
    came = [zeros[d][-1] for d in range(2, planes, 2)]
    pairs[1] = to_quad(
        after(pairs[1], pairs[0], behind["steps1"]), came or zeros[0], behind["steps1"]
    )
    bit = 2
    while bit < planes:
        sent = totals(zeros, bit)
        behind["steps1"].extend(sent.values())
        halve(zeros, bit, sent)
        bit *= 2
    ones = steps(1)
    bit = 1
    while bit < planes:
        sent = totals(ones, bit)
        halve(ones, bit, sent)
        bit *= 2
    got_zero, got_one = zeros[0], ones[0]
    behind["new0"].extend(sent.values())

    sums_shape = (rows, 128)
    step_zero, moved, sums = call(
        first_moved_kernel,
        [(flat, WIDE), (flat, WIDE), (sums_shape, WIDE)],
        0,
        zero,
        *got_zero,
        behind=behind["new0"],
    )
    weights_one, payload = call(
        scaled_kernel, [(flat, WIDE), (flat, LOW)], 0, moved, zero, sums, send(sums, 1)
    )
    full_one = spread(payload)
    queries = to_quad(after(query_tokens, pairs[1], behind["out0"]), [payload], behind["out0"])
    out_zero = returned(readout(0, full_zero))

    decay = jnp.broadcast_to(jnp.where(y == 0, momentum_decay[0], momentum_decay[1]), (8, 128))
    moved, sums = call(
        second_moved_kernel,
        [(flat, WIDE), (sums_shape, WIDE)],
        0,
        weights_one,
        step_zero,
        decay,
        *got_one,
        behind=behind["new1"],
    )
    far_sums = send(sums, 1)
    payload = call(last_scaled_kernel, [(flat, LOW)], 0, moved, weights_one, sums, far_sums)[0]
    full_two = spread_on(spread(payload))
    full_one = spread_on(full_one, [payload], behind["out2"])
    behind["out1"].extend([out_zero, full_two[planes // 2]])
    total_one = readout(1, full_one)
    behind["out2"].append(total_one)
    out_one = returned(total_one)
    out_two = returned(readout(2, full_two))
    return jnp.stack([out_zero, out_one, out_two])


def solution(mesh):
    groups, count = mesh.shape["groups"], mesh.shape["tok"]
    split = Mesh(mesh.devices.reshape(groups, count // 4, 4), ("groups", "plane", "quad"))
    everywhere = P(None, ("groups", "plane", "quad"), None)
    rows = P(None, ("plane", "quad"), None)
    return jax.shard_map(
        shards,
        mesh=split,
        in_specs=(everywhere,) * 4 + (rows,) * 3 + (P(),),
        out_specs=everywhere,
        check_vma=False,
    )
```

```python
import functools

import jax
import jax.numpy as jnp
from jax import lax
from jax.experimental import pallas as pl
from jax.experimental.pallas import tpu as pltpu
from jax.sharding import Mesh, PartitionSpec as P

LOW = jnp.bfloat16
WIDE = jnp.float32


def call(kernel, outs, flops, *operands, scratch=(), behind=()):
    inner, used = kernel, len(operands)

    def kernel(*refs):
        inner(*refs[:used], *refs[used + len(behind) :])

    shapes = [jax.ShapeDtypeStruct(s, d) for s, d in outs]
    return pl.pallas_call(
        kernel,
        out_shape=shapes,
        in_specs=[
            pl.BlockSpec(memory_space=pltpu.SMEM if a.ndim == 1 else pltpu.VMEM) for a in operands
        ]
        + [pl.BlockSpec(memory_space=pl.ANY)] * len(behind),
        out_specs=[pl.BlockSpec(memory_space=pltpu.VMEM)] * len(shapes),
        scratch_shapes=[pltpu.VMEM(s, d) for s, d in scratch],
        compiler_params=pltpu.CompilerParams(vmem_limit_bytes=20 * 2**20),
        cost_estimate=pl.CostEstimate(flops=flops, bytes_accessed=1024, transcendentals=0),
    )(*operands, *behind)


def after(value, others, sink):
    value, others = lax.optimization_barrier((value, list(others)))
    sink.extend(others)
    return value


def dot(a, b, dims):
    return lax.dot_general(a, b, ((dims[:1], dims[1:]), ((), ())), preferred_element_type=WIDE)


def place(pieces, where, first, third, second):
    rows, columns = pieces[0].shape
    width = columns // 3
    half = width // 2
    for distance, piece in enumerate(pieces):
        z = where[0] ^ distance
        at = pl.multiple_of(z * rows, rows)
        first[pl.ds(at, rows), :] = piece[:, :width]
        third[pl.ds(at, rows), :] = piece[:, width : 2 * width]
        for y in range(2):
            start = 2 * width + y * half
            at = pl.multiple_of((2 * z + y) * rows, rows)
            second[pl.ds(at, rows), :] = piece[:, start : start + half]


def steps_kernel(planes, where, *refs):
    pieces, parts, refs = refs[:planes], refs[planes : planes + 4], refs[planes + 4 :]
    sent, (first, third, second, new_first, new_third, new_second) = refs[:planes], refs[planes:]
    rows, columns = pieces[0].shape
    width = columns // 3
    half = width // 2
    place(pieces, where, first, third, second)
    keys = jnp.concatenate([p[0] for p in parts], axis=0)
    scaled = jnp.concatenate([p[1] for p in parts], axis=0)
    pre_gate = dot(keys, first[...], (1, 1))
    pre_up = dot(keys, third[...], (1, 1))
    back = dot(scaled, second[...], (1, 0))
    sig_gate = jax.nn.sigmoid(pre_gate)
    silu = pre_gate * sig_gate
    hidden = (silu * pre_up).astype(LOW)
    d_gate = (back * pre_up * sig_gate * (1.0 + pre_gate * (1.0 - sig_gate))).astype(LOW)
    d_up = (back * silu).astype(LOW)
    new_first[...] = dot(d_gate, keys, (0, 0))
    new_third[...] = dot(d_up, keys, (0, 0))
    new_second[...] = dot(scaled, hidden, (0, 0))
    for distance, out in enumerate(sent):
        z = where[0] ^ distance
        at = pl.ds(pl.multiple_of(z * rows, rows), rows)
        out[:, :width] = new_first[at, :].astype(out.dtype)
        out[:, width : 2 * width] = new_third[at, :].astype(out.dtype)
        for y in range(2):
            start = 2 * width + y * half
            at = pl.ds(pl.multiple_of((2 * z + y) * rows, rows), rows)
            out[:, start : start + half] = new_second[at, :].astype(out.dtype)


def readout_kernel(planes, block, where, *refs):
    pieces, parts, refs = refs[:planes], refs[planes : planes + 4], refs[planes + 4 :]
    kept, sent, first, third, second = refs
    tokens = kept.shape[0] // 2
    place(pieces, where, first, third, second)
    inputs = jnp.concatenate([p[block] for p in parts], axis=0)
    pre_gate = dot(inputs, first[...], (1, 1))
    pre_up = dot(inputs, third[...], (1, 1))
    hidden = (pre_gate * jax.nn.sigmoid(pre_gate) * pre_up).astype(LOW)
    result = dot(hidden, second[...], (1, 1))
    kept[...] = result[: 2 * tokens]
    sent[...] = result[2 * tokens :].astype(LOW)


def square_sums(array, width):
    half = width // 2
    columns = []
    for y in range(2):
        piece = array[:, 2 * width + y * half : 2 * width + (y + 1) * half]
        columns.append(jnp.sum(piece * piece, axis=1, keepdims=True))
    return columns


def moved_kernel(got, old, momentum, decay, new_momentum, moved, sums):
    rows, columns = old.shape
    width = columns // 3
    total = got[0][...].astype(WIDE)
    for part in got[1:]:
        total = total + part[...].astype(WIDE)
    before = old[...].astype(WIDE)
    if momentum is not None:
        total = decay[0:1, 0:1] * momentum[...] + total
    after = before + total
    if new_momentum is not None:
        new_momentum[...] = total
    moved[...] = after
    parts = square_sums(after, width) + square_sums(before, width)
    sums[...] = jnp.concatenate(parts + [jnp.zeros((rows, 124), WIDE)], axis=1)


def first_moved_kernel(old, *refs):
    moved_kernel(refs[:-3], old, None, None, *refs[-3:])


def second_moved_kernel(old, momentum, decay, *refs):
    moved_kernel(refs[:-2], old, momentum, decay, None, *refs[-2:])


def scaled_kernel(moved, old, own_sums, far_sums, new, payload):
    rows, columns = payload.shape
    width = columns // 3
    half = width // 2
    after = moved[...]
    before = old[...].astype(WIDE)
    sums = own_sums[...] + far_sums[...]

    def factor(old_sum, moved_sum):
        return jnp.sqrt(old_sum + 1e-06) / jnp.sqrt(moved_sum + 1e-06)

    pieces = []
    for m in range(2):
        a = after[:, m * width : (m + 1) * width]
        b = before[:, m * width : (m + 1) * width]
        old_sum = jnp.sum(b * b, axis=1, keepdims=True)
        pieces.append(a * factor(old_sum, jnp.sum(a * a, axis=1, keepdims=True)))
    for y in range(2):
        a = after[:, 2 * width + y * half : 2 * width + (y + 1) * half]
        pieces.append(a * factor(sums[:, y + 2 : y + 3], sums[:, y : y + 1]))
    result = jnp.concatenate(pieces, axis=1)
    if new is not None:
        new[...] = result
    payload[...] = result.astype(LOW)


def last_scaled_kernel(moved, old, own_sums, far_sums, payload):
    scaled_kernel(moved, old, own_sums, far_sums, None, payload)


def shards(
    query_tokens,
    key_tokens,
    value_tokens,
    learn_rates,
    fast_first,
    fast_third,
    fast_second,
    momentum_decay,
):
    planes = lax.axis_size("plane")
    index = lax.axis_index("quad")
    y, c = index // 2, index % 2
    width = fast_first.shape[2]
    half = width // 2
    own_rows = fast_first.shape[1]
    rows = 2 * own_rows
    tokens = key_tokens.shape[1]

    def send(array, offset):
        return lax.ppermute(array, "quad", [(q, q ^ offset) for q in range(4)])

    def to_plane(array, bit):
        return lax.ppermute(array, "plane", [(z, z ^ bit) for z in range(planes)])

    def spread(own):
        return {0: own, planes // 2: to_plane(own, planes // 2)}

    def spread_on(pieces, gate, sink):
        bit = planes // 4
        while bit:
            direct = to_plane(pieces[0], bit)
            for distance in list(pieces):
                if distance:
                    piece = after(pieces[distance], [direct] + gate, sink)
                    pieces[distance | bit] = to_plane(piece, bit)
            pieces[bit] = direct
            bit //= 2
        return [pieces[d] for d in range(planes)]

    def totals(parts, bit):
        return {
            d: sum(p.astype(WIDE) for p in parts[d]).astype(LOW)
            for d in range(planes - bit, 0, -2 * bit)
        }

    def halve(parts, bit, sent, sink):
        came = []
        for distance, total in sent.items():
            if distance == bit and came:
                total = after(total, came[-1:], sink)
            came.append(to_plane(total, bit))
            parts[distance ^ bit].append(came[-1])

    def pick(flag, a, b):
        return jnp.where(flag == 0, a, b), jnp.where(flag == 0, b, a)

    def ordered(flag, a, b, axis):
        return jnp.where(flag == 0, jnp.concatenate([a, b], axis), jnp.concatenate([b, a], axis))

    def to_quad(array, gate=None, sink=None):
        mine, other = pick(y, array[..., :width], array[..., width:])
        far = send(other, 2)
        passed = far if gate is None else after(far, gate, sink)
        return mine, far, send(mine, 1), send(passed, 1)

    columns = fast_second.reshape(2, own_rows, 2 * planes, 2, own_rows)
    split = [columns[:, :, :, i].reshape(2, own_rows, half) for i in range(2)]
    second_same, second_other = pick(c, split[0], split[1])
    same = jnp.concatenate([fast_first, fast_third, second_same], axis=2)
    same_mine, same_far = pick(y, same[0], same[1])
    near_mine, near_far = pick(y, second_other[0], second_other[1])
    same_far = send(same_far, 2)
    near_mine, near_far = send(near_mine, 1), send(near_far, 3)
    layers = ordered(y, same_mine[:, : 2 * width], same_far[:, : 2 * width], 0)
    second_mine = ordered(c, same_mine[:, 2 * width :], near_mine, 0)
    second_far = ordered(c, same_far[:, 2 * width :], near_far, 0)
    zero = jnp.concatenate([layers, ordered(y, second_mine, second_far, 1)], axis=1)
    names = ("steps0", "steps1", "out0", "new0", "new1", "out1", "out2")
    behind = {name: [] for name in names}
    full_zero = spread_on(spread(zero), [], behind["steps0"])

    scaled = learn_rates[:2, :, :, None] * value_tokens[:2].reshape(2, tokens, 2, width).astype(WIDE)
    scaled = scaled.astype(LOW).reshape(2, tokens, 2 * width)
    pairs = [jnp.stack([key_tokens[b], scaled[b]]) for b in range(2)]
    flat = (rows, 3 * width)
    unit = 2 * 4 * tokens * width * half
    where = lax.axis_index("plane").astype(jnp.int32).reshape(1)
    held = [((half, width), LOW), ((half, width), LOW), ((width, half), LOW)]

    def steps(block):
        kernel = functools.partial(steps_kernel, planes)
        outs = [(flat, WIDE if d % 2 == 0 else LOW) for d in range(planes)]
        made = [(s, WIDE) for s, _ in held]
        made = call(
            kernel,
            outs,
            6 * unit,
            where,
            *full_zero,
            *pairs[block],
            scratch=held + made,
            behind=behind["steps%d" % block],
        )
        return [[part] for part in made]

    def readout(block, full):
        kernel = functools.partial(readout_kernel, planes, block)
        outs = [((2 * tokens, width), WIDE), ((2 * tokens, width), LOW)]
        kept, sent = call(
            kernel,
            outs,
            3 * unit,
            where,
            *full,
            *queries,
            scratch=held,
            behind=behind["out%d" % block],
        )
        return (kept + send(sent, 1).astype(WIDE)).astype(LOW)

    def returned(total):
        return ordered(y, total[:tokens], send(total[tokens:], 2), 1)

    pairs[0] = to_quad(
        after(pairs[0], [zero], behind["new0"]),
        [full_zero[1], full_zero[planes // 2]],
        behind["steps0"],
    )
    zeros = steps(0)
    halve(zeros, 1, totals(zeros, 1), behind["new0"])
    came = [zeros[d][-1] for d in range(2, planes, 2)]
    pairs[1] = to_quad(
        after(pairs[1], pairs[0], behind["steps1"]), came or zeros[0], behind["steps1"]
    )
    bit = 2
    while bit < planes:
        sent = totals(zeros, bit)
        behind["steps1"].extend(sent.values())
        halve(zeros, bit, sent, behind["new0"])
        bit *= 2
    ones = steps(1)
    bit = 1
    while bit < planes:
        sent = totals(ones, bit)
        halve(ones, bit, sent, behind["new1"])
        bit *= 2
    got_zero, got_one = zeros[0], ones[0]
    behind["new0"].extend(sent.values())

    sums_shape = (rows, 128)
    step_zero, moved, sums = call(
        first_moved_kernel,
        [(flat, WIDE), (flat, WIDE), (sums_shape, WIDE)],
        0,
        zero,
        *got_zero,
        behind=behind["new0"],
    )
    weights_one, payload = call(
        scaled_kernel, [(flat, WIDE), (flat, LOW)], 0, moved, zero, sums, send(sums, 1)
    )
    full_one = spread_on(spread(payload), [], behind["out1"])
    behind["new1"].extend([full_one[1], full_one[planes // 2]])

    decay = jnp.broadcast_to(jnp.where(y == 0, momentum_decay[0], momentum_decay[1]), (8, 128))
    moved, sums = call(
        second_moved_kernel,
        [(flat, WIDE), (sums_shape, WIDE)],
        0,
        weights_one,
        step_zero,
        decay,
        *got_one,
        behind=behind["new1"],
    )
    far_sums = send(sums, 1)
    payload = call(last_scaled_kernel, [(flat, LOW)], 0, moved, weights_one, sums, far_sums)[0]
    full_two = spread_on(spread(payload), [], behind["out2"])
    queries = to_quad(
        after(query_tokens, pairs[1], behind["out0"]), [weights_one], behind["out0"]
    )
    behind["out0"].extend([full_one[planes - 1], full_two[1], full_two[planes // 2]])
    out_zero = returned(readout(0, full_zero))
    behind["out1"].extend([out_zero, full_two[planes - 1]])
    total_one = readout(1, full_one)
    behind["out2"].append(total_one)
    out_one = returned(total_one)
    out_two = returned(readout(2, full_two))
    return jnp.stack([out_zero, out_one, out_two])


def solution(mesh):
    groups, count = mesh.shape["groups"], mesh.shape["tok"]
    split = Mesh(mesh.devices.reshape(groups, count // 4, 4), ("groups", "plane", "quad"))
    everywhere = P(None, ("groups", "plane", "quad"), None)
    rows = P(None, ("plane", "quad"), None)
    return jax.shard_map(
        shards,
        mesh=split,
        in_specs=(everywhere,) * 4 + (rows,) * 3 + (P(),),
        out_specs=everywhere,
        check_vma=False,
    )
```

```python
import functools

import jax
import jax.numpy as jnp
from jax import lax
from jax.experimental import pallas as pl
from jax.experimental.pallas import tpu as pltpu
from jax.sharding import Mesh, PartitionSpec as P

LOW = jnp.bfloat16
WIDE = jnp.float32


def call(kernel, outs, flops, *operands, scratch=(), behind=()):
    inner, used = kernel, len(operands)

    def kernel(*refs):
        inner(*refs[:used], *refs[used + len(behind) :])

    shapes = [jax.ShapeDtypeStruct(s, d) for s, d in outs]
    return pl.pallas_call(
        kernel,
        out_shape=shapes,
        in_specs=[
            pl.BlockSpec(memory_space=pltpu.SMEM if a.ndim == 1 else pltpu.VMEM) for a in operands
        ]
        + [pl.BlockSpec(memory_space=pl.ANY)] * len(behind),
        out_specs=[pl.BlockSpec(memory_space=pltpu.VMEM)] * len(shapes),
        scratch_shapes=[pltpu.VMEM(s, d) for s, d in scratch],
        compiler_params=pltpu.CompilerParams(vmem_limit_bytes=20 * 2**20),
        cost_estimate=pl.CostEstimate(flops=flops, bytes_accessed=1024, transcendentals=0),
    )(*operands, *behind)


def after(value, others, sink):
    value, others = lax.optimization_barrier((value, list(others)))
    sink.extend(others)
    return value


def dot(a, b, dims):
    return lax.dot_general(a, b, ((dims[:1], dims[1:]), ((), ())), preferred_element_type=WIDE)


def place(pieces, where, first, third, second):
    rows, columns = pieces[0].shape
    width = columns // 3
    half = width // 2
    for distance, piece in enumerate(pieces):
        z = where[0] ^ distance
        at = pl.multiple_of(z * rows, rows)
        first[pl.ds(at, rows), :] = piece[:, :width]
        third[pl.ds(at, rows), :] = piece[:, width : 2 * width]
        for y in range(2):
            start = 2 * width + y * half
            at = pl.multiple_of((2 * z + y) * rows, rows)
            second[pl.ds(at, rows), :] = piece[:, start : start + half]


def steps_kernel(planes, where, *refs):
    pieces, parts, refs = refs[:planes], refs[planes : planes + 4], refs[planes + 4 :]
    sent, (first, third, second, new_first, new_third, new_second) = refs[:planes], refs[planes:]
    rows, columns = pieces[0].shape
    width = columns // 3
    half = width // 2
    place(pieces, where, first, third, second)
    keys = jnp.concatenate([p[0] for p in parts], axis=0)
    scaled = jnp.concatenate([p[1] for p in parts], axis=0)
    pre_gate = dot(keys, first[...], (1, 1))
    pre_up = dot(keys, third[...], (1, 1))
    back = dot(scaled, second[...], (1, 0))
    sig_gate = jax.nn.sigmoid(pre_gate)
    silu = pre_gate * sig_gate
    hidden = (silu * pre_up).astype(LOW)
    d_gate = (back * pre_up * sig_gate * (1.0 + pre_gate * (1.0 - sig_gate))).astype(LOW)
    d_up = (back * silu).astype(LOW)
    new_first[...] = dot(d_gate, keys, (0, 0))
    new_third[...] = dot(d_up, keys, (0, 0))
    new_second[...] = dot(scaled, hidden, (0, 0))
    for distance, out in enumerate(sent):
        z = where[0] ^ distance
        at = pl.ds(pl.multiple_of(z * rows, rows), rows)
        out[:, :width] = new_first[at, :].astype(out.dtype)
        out[:, width : 2 * width] = new_third[at, :].astype(out.dtype)
        for y in range(2):
            start = 2 * width + y * half
            at = pl.ds(pl.multiple_of((2 * z + y) * rows, rows), rows)
            out[:, start : start + half] = new_second[at, :].astype(out.dtype)


def readout_kernel(planes, block, where, *refs):
    pieces, parts, refs = refs[:planes], refs[planes : planes + 4], refs[planes + 4 :]
    kept, sent, first, third, second = refs
    tokens = kept.shape[0] // 2
    place(pieces, where, first, third, second)
    inputs = jnp.concatenate([p[block] for p in parts], axis=0)
    pre_gate = dot(inputs, first[...], (1, 1))
    pre_up = dot(inputs, third[...], (1, 1))
    hidden = (pre_gate * jax.nn.sigmoid(pre_gate) * pre_up).astype(LOW)
    result = dot(hidden, second[...], (1, 1))
    kept[...] = result[: 2 * tokens]
    sent[...] = result[2 * tokens :].astype(LOW)


def square_sums(array, width):
    half = width // 2
    columns = []
    for y in range(2):
        piece = array[:, 2 * width + y * half : 2 * width + (y + 1) * half]
        columns.append(jnp.sum(piece * piece, axis=1, keepdims=True))
    return columns


def moved_kernel(got, old, momentum, decay, new_momentum, moved, sums):
    rows, columns = old.shape
    width = columns // 3
    total = got[0][...].astype(WIDE)
    for part in got[1:]:
        total = total + part[...].astype(WIDE)
    before = old[...].astype(WIDE)
    if momentum is not None:
        total = decay[0:1, 0:1] * momentum[...] + total
    after = before + total
    if new_momentum is not None:
        new_momentum[...] = total
    moved[...] = after
    parts = square_sums(after, width) + square_sums(before, width)
    sums[...] = jnp.concatenate(parts + [jnp.zeros((rows, 124), WIDE)], axis=1)


def first_moved_kernel(old, *refs):
    moved_kernel(refs[:-3], old, None, None, *refs[-3:])


def second_moved_kernel(old, momentum, decay, *refs):
    moved_kernel(refs[:-2], old, momentum, decay, None, *refs[-2:])


def scaled_kernel(moved, old, own_sums, far_sums, new, payload):
    rows, columns = payload.shape
    width = columns // 3
    half = width // 2
    after = moved[...]
    before = old[...].astype(WIDE)
    sums = own_sums[...] + far_sums[...]

    def factor(old_sum, moved_sum):
        return jnp.sqrt(old_sum + 1e-06) / jnp.sqrt(moved_sum + 1e-06)

    pieces = []
    for m in range(2):
        a = after[:, m * width : (m + 1) * width]
        b = before[:, m * width : (m + 1) * width]
        old_sum = jnp.sum(b * b, axis=1, keepdims=True)
        pieces.append(a * factor(old_sum, jnp.sum(a * a, axis=1, keepdims=True)))
    for y in range(2):
        a = after[:, 2 * width + y * half : 2 * width + (y + 1) * half]
        pieces.append(a * factor(sums[:, y + 2 : y + 3], sums[:, y : y + 1]))
    result = jnp.concatenate(pieces, axis=1)
    if new is not None:
        new[...] = result
    payload[...] = result.astype(LOW)


def last_scaled_kernel(moved, old, own_sums, far_sums, payload):
    scaled_kernel(moved, old, own_sums, far_sums, None, payload)


def shards(
    query_tokens,
    key_tokens,
    value_tokens,
    learn_rates,
    fast_first,
    fast_third,
    fast_second,
    momentum_decay,
):
    planes = lax.axis_size("plane")
    index = lax.axis_index("quad")
    y, c = index // 2, index % 2
    width = fast_first.shape[2]
    half = width // 2
    own_rows = fast_first.shape[1]
    rows = 2 * own_rows
    tokens = key_tokens.shape[1]

    def send(array, offset):
        return lax.ppermute(array, "quad", [(q, q ^ offset) for q in range(4)])

    def to_plane(array, bit):
        return lax.ppermute(array, "plane", [(z, z ^ bit) for z in range(planes)])

    def spread(own):
        return {0: own, planes // 2: to_plane(own, planes // 2)}

    def spread_on(pieces, sink=None):
        bit = planes // 4
        while bit:
            direct = to_plane(pieces[0], bit)
            for distance in list(pieces):
                if distance:
                    piece = pieces[distance]
                    if sink is not None:
                        piece = after(piece, [direct], sink)
                    pieces[distance | bit] = to_plane(piece, bit)
            pieces[bit] = direct
            bit //= 2
        return [pieces[d] for d in range(planes)]

    def totals(parts, bit):
        return {
            d: sum(p.astype(WIDE) for p in parts[d]).astype(LOW)
            for d in range(planes - bit, 0, -2 * bit)
        }

    def halve(parts, bit, sent):
        relayed = None
        for distance, total in sent.items():
            if distance == bit and relayed is not None:
                total, came = lax.optimization_barrier((total, parts[relayed][-1]))
                parts[relayed][-1] = came
            parts[distance ^ bit].append(to_plane(total, bit))
            relayed = distance ^ bit

    def pick(flag, a, b):
        return jnp.where(flag == 0, a, b), jnp.where(flag == 0, b, a)

    def ordered(flag, a, b, axis):
        return jnp.where(flag == 0, jnp.concatenate([a, b], axis), jnp.concatenate([b, a], axis))

    def to_quad(array, gate=None, sink=None):
        mine, other = pick(y, array[..., :width], array[..., width:])
        far = send(other, 2)
        passed = far if gate is None else after(far, gate, sink)
        return mine, far, send(mine, 1), send(passed, 1)

    columns = fast_second.reshape(2, own_rows, 2 * planes, 2, own_rows)
    split = [columns[:, :, :, i].reshape(2, own_rows, half) for i in range(2)]
    second_same, second_other = pick(c, split[0], split[1])
    same = jnp.concatenate([fast_first, fast_third, second_same], axis=2)
    same_mine, same_far = pick(y, same[0], same[1])
    near_mine, near_far = pick(y, second_other[0], second_other[1])
    same_far = send(same_far, 2)
    near_mine, near_far = send(near_mine, 1), send(near_far, 3)
    layers = ordered(y, same_mine[:, : 2 * width], same_far[:, : 2 * width], 0)
    second_mine = ordered(c, same_mine[:, 2 * width :], near_mine, 0)
    second_far = ordered(c, same_far[:, 2 * width :], near_far, 0)
    zero = jnp.concatenate([layers, ordered(y, second_mine, second_far, 1)], axis=1)
    names = ("steps0", "steps1", "out0", "new0", "new1", "out1", "out2")
    behind = {name: [] for name in names}
    full_zero = spread_on(spread(zero), behind["steps0"])

    scaled = learn_rates[:2, :, :, None] * value_tokens[:2].reshape(2, tokens, 2, width).astype(WIDE)
    scaled = scaled.astype(LOW).reshape(2, tokens, 2 * width)
    pairs = [jnp.stack([key_tokens[b], scaled[b]]) for b in range(2)]
    flat = (rows, 3 * width)
    unit = 2 * 4 * tokens * width * half
    where = lax.axis_index("plane").astype(jnp.int32).reshape(1)
    held = [((half, width), LOW), ((half, width), LOW), ((width, half), LOW)]

    def steps(block):
        kernel = functools.partial(steps_kernel, planes)
        outs = [(flat, WIDE if d % 2 == 0 else LOW) for d in range(planes)]
        made = [(s, WIDE) for s, _ in held]
        made = call(
            kernel,
            outs,
            6 * unit,
            where,
            *full_zero,
            *pairs[block],
            scratch=held + made,
            behind=behind["steps%d" % block],
        )
        return [[part] for part in made]

    def readout(block, full):
        kernel = functools.partial(readout_kernel, planes, block)
        outs = [((2 * tokens, width), WIDE), ((2 * tokens, width), LOW)]
        kept, sent = call(
            kernel,
            outs,
            3 * unit,
            where,
            *full,
            *queries,
            scratch=held,
            behind=behind["out%d" % block],
        )
        return (kept + send(sent, 1).astype(WIDE)).astype(LOW)

    def returned(total):
        return ordered(y, total[:tokens], send(total[tokens:], 2), 1)

    pairs[0] = to_quad(
        after(pairs[0], [zero], behind["new0"]),
        [full_zero[1], full_zero[planes // 2]],
        behind["steps0"],
    )
    zeros = steps(0)
    halve(zeros, 1, totals(zeros, 1))
    came = [zeros[d][-1] for d in range(2, planes, 2)]
    pairs[1] = to_quad(
        after(pairs[1], pairs[0], behind["steps1"]), came or zeros[0], behind["steps1"]
    )
    bit = 2
    while bit < planes:
        sent = totals(zeros, bit)
        behind["steps1"].extend(sent.values())
        halve(zeros, bit, sent)
        bit *= 2
    ones = steps(1)
    bit = 1
    while bit < planes:
        sent = totals(ones, bit)
        halve(ones, bit, sent)
        bit *= 2
    got_zero, got_one = zeros[0], ones[0]
    behind["new0"].extend(sent.values())

    sums_shape = (rows, 128)
    step_zero, moved, sums = call(
        first_moved_kernel,
        [(flat, WIDE), (flat, WIDE), (sums_shape, WIDE)],
        0,
        zero,
        *got_zero,
        behind=behind["new0"],
    )
    weights_one, payload = call(
        scaled_kernel, [(flat, WIDE), (flat, LOW)], 0, moved, zero, sums, send(sums, 1)
    )
    first_one = spread(payload)
    direct_one = to_plane(payload, 1)
    queries = to_quad(
        after(query_tokens, pairs[1], behind["out0"]), [weights_one], behind["out0"]
    )

    half_way = planes // 2
    waited = (got_one, first_one[half_way], direct_one)
    got_one, first_one[half_way], direct_one = lax.optimization_barrier(waited)
    decay = jnp.broadcast_to(jnp.where(y == 0, momentum_decay[0], momentum_decay[1]), (8, 128))
    moved, sums = call(
        second_moved_kernel,
        [(flat, WIDE), (sums_shape, WIDE)],
        0,
        weights_one,
        step_zero,
        decay,
        *got_one,
        behind=behind["new1"],
    )
    far_sums = send(sums, 1)
    payload = call(last_scaled_kernel, [(flat, LOW)], 0, moved, weights_one, sums, far_sums)[0]
    first_two = spread(payload)
    direct_two = to_plane(payload, 1)
    full_one = spread_on(first_one)
    full_one[1] = direct_one
    waited = (first_two[half_way], direct_two, queries[0], full_one[planes - 1])
    first_two[half_way], direct_two, first_query, full_one[planes - 1] = (
        lax.optimization_barrier(waited)
    )
    queries = (first_query,) + queries[1:]
    full_two = spread_on(first_two)
    full_two[1] = direct_two
    out_zero = returned(readout(0, full_zero))
    total_one = readout(1, full_one)
    waited = (full_two[planes - 1], out_zero, total_one)
    full_two[planes - 1], out_zero, total_one = lax.optimization_barrier(waited)
    out_one = returned(total_one)
    out_two = returned(readout(2, full_two))
    return jnp.stack([out_zero, out_one, out_two])


def solution(mesh):
    groups, count = mesh.shape["groups"], mesh.shape["tok"]
    split = Mesh(mesh.devices.reshape(groups, count // 4, 4), ("groups", "plane", "quad"))
    everywhere = P(None, ("groups", "plane", "quad"), None)
    rows = P(None, ("plane", "quad"), None)
    return jax.shard_map(
        shards,
        mesh=split,
        in_specs=(everywhere,) * 4 + (rows,) * 3 + (P(),),
        out_specs=everywhere,
        check_vma=False,
    )
```

```python
import functools

import jax
import jax.numpy as jnp
from jax import lax
from jax.experimental import pallas as pl
from jax.experimental.pallas import tpu as pltpu
from jax.sharding import Mesh, PartitionSpec as P

LOW = jnp.bfloat16
WIDE = jnp.float32


def call(kernel, outs, flops, *operands, scratch=(), behind=()):
    inner, used = kernel, len(operands)

    def kernel(*refs):
        inner(*refs[:used], *refs[used + len(behind) :])

    shapes = [jax.ShapeDtypeStruct(s, d) for s, d in outs]
    return pl.pallas_call(
        kernel,
        out_shape=shapes,
        in_specs=[
            pl.BlockSpec(memory_space=pltpu.SMEM if a.ndim == 1 else pltpu.VMEM) for a in operands
        ]
        + [pl.BlockSpec(memory_space=pl.ANY)] * len(behind),
        out_specs=[pl.BlockSpec(memory_space=pltpu.VMEM)] * len(shapes),
        scratch_shapes=[pltpu.VMEM(s, d) for s, d in scratch],
        compiler_params=pltpu.CompilerParams(vmem_limit_bytes=20 * 2**20),
        cost_estimate=pl.CostEstimate(flops=flops, bytes_accessed=1024, transcendentals=0),
    )(*operands, *behind)


def after(value, others, sink):
    value, others = lax.optimization_barrier((value, list(others)))
    sink.extend(others)
    return value


def dot(a, b, dims):
    return lax.dot_general(a, b, ((dims[:1], dims[1:]), ((), ())), preferred_element_type=WIDE)


def place(pieces, where, first, third, second):
    rows, columns = pieces[0].shape
    width = columns // 3
    half = width // 2
    for distance, piece in enumerate(pieces):
        z = where[0] ^ distance
        at = pl.multiple_of(z * rows, rows)
        first[pl.ds(at, rows), :] = piece[:, :width]
        third[pl.ds(at, rows), :] = piece[:, width : 2 * width]
        for y in range(2):
            start = 2 * width + y * half
            at = pl.multiple_of((2 * z + y) * rows, rows)
            second[pl.ds(at, rows), :] = piece[:, start : start + half]


def steps_kernel(planes, where, *refs):
    pieces, parts, refs = refs[:planes], refs[planes : planes + 4], refs[planes + 4 :]
    sent, (first, third, second, new_first, new_third, new_second) = refs[:planes], refs[planes:]
    rows, columns = pieces[0].shape
    width = columns // 3
    half = width // 2
    place(pieces, where, first, third, second)
    keys = jnp.concatenate([p[0] for p in parts], axis=0)
    scaled = jnp.concatenate([p[1] for p in parts], axis=0)
    pre_gate = dot(keys, first[...], (1, 1))
    pre_up = dot(keys, third[...], (1, 1))
    back = dot(scaled, second[...], (1, 0))
    sig_gate = jax.nn.sigmoid(pre_gate)
    silu = pre_gate * sig_gate
    hidden = (silu * pre_up).astype(LOW)
    d_gate = (back * pre_up * sig_gate * (1.0 + pre_gate * (1.0 - sig_gate))).astype(LOW)
    d_up = (back * silu).astype(LOW)
    new_first[...] = dot(d_gate, keys, (0, 0))
    new_third[...] = dot(d_up, keys, (0, 0))
    new_second[...] = dot(scaled, hidden, (0, 0))
    for distance, out in enumerate(sent):
        z = where[0] ^ distance
        at = pl.ds(pl.multiple_of(z * rows, rows), rows)
        out[:, :width] = new_first[at, :].astype(out.dtype)
        out[:, width : 2 * width] = new_third[at, :].astype(out.dtype)
        for y in range(2):
            start = 2 * width + y * half
            at = pl.ds(pl.multiple_of((2 * z + y) * rows, rows), rows)
            out[:, start : start + half] = new_second[at, :].astype(out.dtype)


def readout_kernel(planes, block, where, *refs):
    pieces, parts, refs = refs[:planes], refs[planes : planes + 4], refs[planes + 4 :]
    kept, sent, first, third, second = refs
    tokens = kept.shape[0] // 2
    place(pieces, where, first, third, second)
    inputs = jnp.concatenate([p[block] for p in parts], axis=0)
    pre_gate = dot(inputs, first[...], (1, 1))
    pre_up = dot(inputs, third[...], (1, 1))
    hidden = (pre_gate * jax.nn.sigmoid(pre_gate) * pre_up).astype(LOW)
    result = dot(hidden, second[...], (1, 1))
    kept[...] = result[: 2 * tokens]
    sent[...] = result[2 * tokens :].astype(LOW)


def square_sums(array, width):
    half = width // 2
    columns = []
    for y in range(2):
        piece = array[:, 2 * width + y * half : 2 * width + (y + 1) * half]
        columns.append(jnp.sum(piece * piece, axis=1, keepdims=True))
    return columns


def sums_of(array, width):
    parts = [array[:, m * width : (m + 1) * width] for m in range(2)]
    parts = [jnp.sum(p * p, axis=1, keepdims=True) for p in parts] + square_sums(array, width)
    return jnp.concatenate(parts + [jnp.zeros((array.shape[0], 124), WIDE)], axis=1)


def first_moved_kernel(old, *refs):
    got, (momentum, moved, sums) = refs[:-3], refs[-3:]
    rows, width = old.shape[0], old.shape[1] // 3
    total = got[0][...].astype(WIDE)
    for part in got[1:]:
        total = total + part[...].astype(WIDE)
    before = old[...].astype(WIDE)
    after_step = before + total
    momentum[...] = total
    moved[...] = after_step
    sums[:rows, :] = sums_of(after_step, width)
    sums[rows:, :] = sums_of(before, width)


def second_moved_kernel(base, *refs):
    got, (moved, sums) = refs[:-2], refs[-2:]
    total = base[...]
    for part in got:
        total = total + part[...].astype(WIDE)
    moved[...] = total
    sums[...] = sums_of(total, total.shape[1] // 3)


def factors(sums, far_sums, old_sums, far_old_sums):
    def whole(mine, far, m):
        return mine[:, m : m + 1] + (far[:, m : m + 1] if m > 1 else 0.0)

    return [
        jnp.sqrt(whole(old_sums, far_old_sums, m) + 1e-06)
        / jnp.sqrt(whole(sums, far_sums, m) + 1e-06)
        for m in range(4)
    ]


def rescaled(moved, scales):
    width = moved.shape[1] // 3
    half = width // 2
    edges = [0, width, 2 * width, 2 * width + half, 3 * width]
    pieces = [moved[:, edges[m] : edges[m + 1]] * scales[m] for m in range(4)]
    return jnp.concatenate(pieces, axis=1)


def scaled_kernel(moved, momentum, decay, part, sums, far, base, payload, new_sums):
    rows = moved.shape[0]
    new, old = slice(0, rows), slice(rows, None)
    result = rescaled(moved, factors(sums[new], far[new], sums[old], far[old]))
    payload[...] = result.astype(LOW)
    new_sums[...] = sums_of(result, result.shape[1] // 3)
    base[...] = result + (decay[0:1, 0:1] * momentum[...] + part[...])


def last_scaled_kernel(moved, sums, far, old, far_old, payload):
    payload[...] = rescaled(moved, factors(sums, far, old, far_old)).astype(LOW)


def shards(
    query_tokens,
    key_tokens,
    value_tokens,
    learn_rates,
    fast_first,
    fast_third,
    fast_second,
    momentum_decay,
):
    planes = lax.axis_size("plane")
    index = lax.axis_index("quad")
    y, c = index // 2, index % 2
    width = fast_first.shape[2]
    half = width // 2
    own_rows = fast_first.shape[1]
    rows = 2 * own_rows
    tokens = key_tokens.shape[1]

    def send(array, offset):
        return lax.ppermute(array, "quad", [(q, q ^ offset) for q in range(4)])

    def to_plane(array, bit):
        return lax.ppermute(array, "plane", [(z, z ^ bit) for z in range(planes)])

    def spread(own):
        return {0: own, planes // 2: to_plane(own, planes // 2)}

    def spread_on(pieces, sink=None):
        bit = planes // 4
        while bit:
            direct = to_plane(pieces[0], bit)
            for distance in list(pieces):
                if distance:
                    piece = pieces[distance]
                    if sink is not None:
                        piece = after(piece, [direct], sink)
                    pieces[distance | bit] = to_plane(piece, bit)
            pieces[bit] = direct
            bit //= 2
        return [pieces[d] for d in range(planes)]

    def totals(parts, bit):
        return {
            d: sum(p.astype(WIDE) for p in parts[d]).astype(LOW)
            for d in range(planes - bit, 0, -2 * bit)
        }

    def halve(parts, bit, sent):
        relayed = None
        for distance, total in sent.items():
            if distance == bit and relayed is not None:
                total, came = lax.optimization_barrier((total, parts[relayed][-1]))
                parts[relayed][-1] = came
            parts[distance ^ bit].append(to_plane(total, bit))
            relayed = distance ^ bit

    def pick(flag, a, b):
        return jnp.where(flag == 0, a, b), jnp.where(flag == 0, b, a)

    def ordered(flag, a, b, axis):
        return jnp.where(flag == 0, jnp.concatenate([a, b], axis), jnp.concatenate([b, a], axis))

    def to_quad(array, gate=None, sink=None):
        mine, other = pick(y, array[..., :width], array[..., width:])
        far = send(other, 2)
        passed = far if gate is None else after(far, gate, sink)
        return mine, far, send(mine, 1), send(passed, 1)

    columns = fast_second.reshape(2, own_rows, 2 * planes, 2, own_rows)
    split = [columns[:, :, :, i].reshape(2, own_rows, half) for i in range(2)]
    second_same, second_other = pick(c, split[0], split[1])
    same = jnp.concatenate([fast_first, fast_third, second_same], axis=2)
    same_mine, same_far = pick(y, same[0], same[1])
    near_mine, near_far = pick(y, second_other[0], second_other[1])
    same_far = send(same_far, 2)
    near_mine, near_far = send(near_mine, 1), send(near_far, 3)
    layers = ordered(y, same_mine[:, : 2 * width], same_far[:, : 2 * width], 0)
    second_mine = ordered(c, same_mine[:, 2 * width :], near_mine, 0)
    second_far = ordered(c, same_far[:, 2 * width :], near_far, 0)
    zero = jnp.concatenate([layers, ordered(y, second_mine, second_far, 1)], axis=1)
    names = ("steps0", "steps1", "out0", "new0", "new1", "out1", "out2")
    behind = {name: [] for name in names}
    full_zero = spread_on(spread(zero), behind["steps0"])

    scaled = learn_rates[:2, :, :, None] * value_tokens[:2].reshape(2, tokens, 2, width).astype(WIDE)
    scaled = scaled.astype(LOW).reshape(2, tokens, 2 * width)
    pairs = [jnp.stack([key_tokens[b], scaled[b]]) for b in range(2)]
    flat = (rows, 3 * width)
    unit = 2 * 4 * tokens * width * half
    where = lax.axis_index("plane").astype(jnp.int32).reshape(1)
    held = [((half, width), LOW), ((half, width), LOW), ((width, half), LOW)]

    def steps(block):
        kernel = functools.partial(steps_kernel, planes)
        outs = [(flat, WIDE if d % 2 == 0 else LOW) for d in range(planes)]
        made = [(s, WIDE) for s, _ in held]
        made = call(
            kernel,
            outs,
            6 * unit,
            where,
            *full_zero,
            *pairs[block],
            scratch=held + made,
            behind=behind["steps%d" % block],
        )
        return [[part] for part in made]

    def readout(block, full):
        kernel = functools.partial(readout_kernel, planes, block)
        outs = [((2 * tokens, width), WIDE), ((2 * tokens, width), LOW)]
        kept, sent = call(
            kernel,
            outs,
            3 * unit,
            where,
            *full,
            *queries,
            scratch=held,
            behind=behind["out%d" % block],
        )
        return (kept + send(sent, 1).astype(WIDE)).astype(LOW)

    def returned(total):
        return ordered(y, total[:tokens], send(total[tokens:], 2), 1)

    pairs[0] = to_quad(
        after(pairs[0], [zero], behind["new0"]),
        [full_zero[1], full_zero[planes // 2]],
        behind["steps0"],
    )
    zeros = steps(0)
    halve(zeros, 1, totals(zeros, 1))
    came = [zeros[d][-1] for d in range(2, planes, 2)]
    pairs[1] = to_quad(
        after(pairs[1], pairs[0], behind["steps1"]), came or zeros[0], behind["steps1"]
    )
    bit = 2
    while bit < planes:
        sent = totals(zeros, bit)
        behind["steps1"].extend(sent.values())
        halve(zeros, bit, sent)
        bit *= 2
    ones = steps(1)
    bit = 1
    while bit < planes:
        sent = totals(ones, bit)
        halve(ones, bit, sent)
        bit *= 2
    got_zero, got_one = zeros[0], ones[0]
    behind["new0"].extend(sent.values())

    sums_shape = (rows, 128)
    flat_sums = [(sums_shape, WIDE)]
    step_zero, moved, sums = call(
        first_moved_kernel,
        [(flat, WIDE), (flat, WIDE), ((2 * rows, 128), WIDE)],
        0,
        zero,
        *got_zero,
        behind=behind["new0"],
    )
    decay = jnp.broadcast_to(jnp.where(y == 0, momentum_decay[0], momentum_decay[1]), (8, 128))
    base, payload, old_sums = call(
        scaled_kernel,
        [(flat, WIDE), (flat, LOW)] + flat_sums,
        0,
        moved,
        step_zero,
        decay,
        got_one[0],
        sums,
        send(sums, 1),
    )
    half_way = planes // 2
    first_one = spread(payload)
    direct_one = to_plane(payload, 1)
    queries = to_quad(
        after(query_tokens, pairs[1], behind["out0"]), [old_sums], behind["out0"]
    )
    far_old = send(old_sums, 1)
    moved, sums = call(
        second_moved_kernel,
        [(flat, WIDE)] + flat_sums,
        0,
        base,
        *got_one[1:],
        behind=behind["new1"],
    )
    waited = (send(sums, 1), first_one[half_way], direct_one)
    far, first_one[half_way], direct_one = lax.optimization_barrier(waited)
    payload = call(last_scaled_kernel, [(flat, LOW)], 0, moved, sums, far, old_sums, far_old)[0]
    first_two = spread(payload)
    direct_two = to_plane(payload, 1)
    full_one = spread_on(first_one)
    full_one[1] = direct_one
    waited = (first_two[half_way], direct_two, queries[0], full_one[planes - 1])
    first_two[half_way], direct_two, first_query, full_one[planes - 1] = (
        lax.optimization_barrier(waited)
    )
    queries = (first_query,) + queries[1:]
    full_two = spread_on(first_two)
    full_two[1] = direct_two
    out_zero = returned(readout(0, full_zero))
    total_one = readout(1, full_one)
    waited = (full_two[planes - 1], out_zero, total_one)
    full_two[planes - 1], out_zero, total_one = lax.optimization_barrier(waited)
    out_one = returned(total_one)
    out_two = returned(readout(2, full_two))
    return jnp.stack([out_zero, out_one, out_two])


def solution(mesh):
    groups, count = mesh.shape["groups"], mesh.shape["tok"]
    split = Mesh(mesh.devices.reshape(groups, count // 4, 4), ("groups", "plane", "quad"))
    everywhere = P(None, ("groups", "plane", "quad"), None)
    rows = P(None, ("plane", "quad"), None)
    return jax.shard_map(
        shards,
        mesh=split,
        in_specs=(everywhere,) * 4 + (rows,) * 3 + (P(),),
        out_specs=everywhere,
        check_vma=False,
    )
```

```python
import functools

import jax
import jax.numpy as jnp
from jax import lax
from jax.experimental import pallas as pl
from jax.experimental.pallas import tpu as pltpu
from jax.sharding import Mesh, PartitionSpec as P

LOW = jnp.bfloat16
WIDE = jnp.float32


def call(kernel, outs, flops, *operands, scratch=(), behind=()):
    inner, used = kernel, len(operands)

    def kernel(*refs):
        inner(*refs[:used], *refs[used + len(behind) :])

    shapes = [jax.ShapeDtypeStruct(s, d) for s, d in outs]
    return pl.pallas_call(
        kernel,
        out_shape=shapes,
        in_specs=[
            pl.BlockSpec(memory_space=pltpu.SMEM if a.ndim == 1 else pltpu.VMEM) for a in operands
        ]
        + [pl.BlockSpec(memory_space=pl.ANY)] * len(behind),
        out_specs=[pl.BlockSpec(memory_space=pltpu.VMEM)] * len(shapes),
        scratch_shapes=[pltpu.VMEM(s, d) for s, d in scratch],
        compiler_params=pltpu.CompilerParams(vmem_limit_bytes=20 * 2**20),
        cost_estimate=pl.CostEstimate(flops=flops, bytes_accessed=1024, transcendentals=0),
    )(*operands, *behind)


def after(value, others, sink):
    value, others = lax.optimization_barrier((value, list(others)))
    sink.extend(others)
    return value


def dot(a, b, dims):
    return lax.dot_general(a, b, ((dims[:1], dims[1:]), ((), ())), preferred_element_type=WIDE)


def place(pieces, where, first, third, second):
    rows, columns = pieces[0].shape
    width = columns // 3
    half = width // 2
    for distance, piece in enumerate(pieces):
        z = where[0] ^ distance
        at = pl.multiple_of(z * rows, rows)
        first[pl.ds(at, rows), :] = piece[:, :width]
        third[pl.ds(at, rows), :] = piece[:, width : 2 * width]
        for y in range(2):
            start = 2 * width + y * half
            at = pl.multiple_of((2 * z + y) * rows, rows)
            second[pl.ds(at, rows), :] = piece[:, start : start + half]


def steps_kernel(planes, where, *refs):
    pieces, parts, refs = refs[:planes], refs[planes : planes + 4], refs[planes + 4 :]
    sent, (first, third, second, new_first, new_third, new_second) = refs[:planes], refs[planes:]
    rows, columns = pieces[0].shape
    width = columns // 3
    half = width // 2
    place(pieces, where, first, third, second)
    keys = jnp.concatenate([p[0] for p in parts], axis=0)
    scaled = jnp.concatenate([p[1] for p in parts], axis=0)
    pre_gate = dot(keys, first[...], (1, 1))
    pre_up = dot(keys, third[...], (1, 1))
    back = dot(scaled, second[...], (1, 0))
    sig_gate = jax.nn.sigmoid(pre_gate)
    silu = pre_gate * sig_gate
    hidden = (silu * pre_up).astype(LOW)
    d_gate = (back * pre_up * sig_gate * (1.0 + pre_gate * (1.0 - sig_gate))).astype(LOW)
    d_up = (back * silu).astype(LOW)
    new_first[...] = dot(d_gate, keys, (0, 0))
    new_third[...] = dot(d_up, keys, (0, 0))
    new_second[...] = dot(scaled, hidden, (0, 0))
    for distance, out in enumerate(sent):
        z = where[0] ^ distance
        at = pl.ds(pl.multiple_of(z * rows, rows), rows)
        out[:, :width] = new_first[at, :].astype(out.dtype)
        out[:, width : 2 * width] = new_third[at, :].astype(out.dtype)
        for y in range(2):
            start = 2 * width + y * half
            at = pl.ds(pl.multiple_of((2 * z + y) * rows, rows), rows)
            out[:, start : start + half] = new_second[at, :].astype(out.dtype)


def readout_kernel(planes, block, where, *refs):
    pieces, parts, refs = refs[:planes], refs[planes : planes + 4], refs[planes + 4 :]
    kept, sent, first, third, second = refs
    tokens = kept.shape[0] // 2
    place(pieces, where, first, third, second)
    inputs = jnp.concatenate([p[block] for p in parts], axis=0)
    pre_gate = dot(inputs, first[...], (1, 1))
    pre_up = dot(inputs, third[...], (1, 1))
    hidden = (pre_gate * jax.nn.sigmoid(pre_gate) * pre_up).astype(LOW)
    result = dot(hidden, second[...], (1, 1))
    kept[...] = result[: 2 * tokens]
    sent[...] = result[2 * tokens :].astype(LOW)


def square_sums(array, width):
    half = width // 2
    columns = []
    for y in range(2):
        piece = array[:, 2 * width + y * half : 2 * width + (y + 1) * half]
        columns.append(jnp.sum(piece * piece, axis=1, keepdims=True))
    return columns


def sums_of(array, width):
    parts = [array[:, m * width : (m + 1) * width] for m in range(2)]
    parts = [jnp.sum(p * p, axis=1, keepdims=True) for p in parts] + square_sums(array, width)
    return jnp.concatenate(parts + [jnp.zeros((array.shape[0], 124), WIDE)], axis=1)


def first_moved_kernel(old, *refs):
    got, (momentum, moved, sums) = refs[:-3], refs[-3:]
    rows, width = old.shape[0], old.shape[1] // 3
    total = got[0][...].astype(WIDE)
    for part in got[1:]:
        total = total + part[...].astype(WIDE)
    before = old[...].astype(WIDE)
    after_step = before + total
    momentum[...] = total
    moved[...] = after_step
    sums[:rows, :] = sums_of(after_step, width)
    sums[rows:, :] = sums_of(before, width)


def second_moved_kernel(base, *refs):
    got, (moved, sums) = refs[:-2], refs[-2:]
    total = base[...]
    for part in got:
        total = total + part[...].astype(WIDE)
    moved[...] = total
    sums[...] = sums_of(total, total.shape[1] // 3)


def factors(sums, far_sums, old_sums, far_old_sums):
    def whole(mine, far, m):
        return mine[:, m : m + 1] + (far[:, m : m + 1] if m > 1 else 0.0)

    return [
        jnp.sqrt(whole(old_sums, far_old_sums, m) + 1e-06)
        / jnp.sqrt(whole(sums, far_sums, m) + 1e-06)
        for m in range(4)
    ]


def rescaled(moved, scales):
    width = moved.shape[1] // 3
    half = width // 2
    edges = [0, width, 2 * width, 2 * width + half, 3 * width]
    pieces = [moved[:, edges[m] : edges[m + 1]] * scales[m] for m in range(4)]
    return jnp.concatenate(pieces, axis=1)


def scaled_kernel(moved, momentum, decay, part, sums, far, base, payload, new_sums):
    rows = moved.shape[0]
    new, old = slice(0, rows), slice(rows, None)
    result = rescaled(moved, factors(sums[new], far[new], sums[old], far[old]))
    payload[...] = result.astype(LOW)
    new_sums[...] = sums_of(result, result.shape[1] // 3)
    base[...] = result + (decay[0:1, 0:1] * momentum[...] + part[...])


def last_scaled_kernel(moved, sums, far, old, far_old, payload):
    payload[...] = rescaled(moved, factors(sums, far, old, far_old)).astype(LOW)


def shards(
    query_tokens,
    key_tokens,
    value_tokens,
    learn_rates,
    fast_first,
    fast_third,
    fast_second,
    momentum_decay,
):
    planes = lax.axis_size("plane")
    index = lax.axis_index("quad")
    y, c = index // 2, index % 2
    width = fast_first.shape[2]
    half = width // 2
    own_rows = fast_first.shape[1]
    rows = 2 * own_rows
    tokens = key_tokens.shape[1]

    def send(array, offset):
        return lax.ppermute(array, "quad", [(q, q ^ offset) for q in range(4)])

    def to_plane(array, bit):
        return lax.ppermute(array, "plane", [(z, z ^ bit) for z in range(planes)])

    def spread(own):
        return {0: own, planes // 2: to_plane(own, planes // 2)}

    def spread_on(pieces, sink=None):
        bit = planes // 4
        while bit:
            direct = to_plane(pieces[0], bit)
            for distance in list(pieces):
                if distance:
                    piece = pieces[distance]
                    if sink is not None:
                        piece = after(piece, [direct], sink)
                    pieces[distance | bit] = to_plane(piece, bit)
            pieces[bit] = direct
            bit //= 2
        return [pieces[d] for d in range(planes)]

    def totals(parts, bit):
        return {
            d: sum(p.astype(WIDE) for p in parts[d]).astype(LOW)
            for d in range(planes - bit, 0, -2 * bit)
        }

    def halve(parts, bit, sent, relayed_first):
        relayed = None
        for distance, total in sent.items():
            if relayed_first and distance == bit and relayed is not None:
                total, came = lax.optimization_barrier((total, parts[relayed][-1]))
                parts[relayed][-1] = came
            parts[distance ^ bit].append(to_plane(total, bit))
            relayed = distance ^ bit

    def pick(flag, a, b):
        return jnp.where(flag == 0, a, b), jnp.where(flag == 0, b, a)

    def ordered(flag, a, b, axis):
        return jnp.where(flag == 0, jnp.concatenate([a, b], axis), jnp.concatenate([b, a], axis))

    def to_quad(array, gate=None, sink=None):
        mine, other = pick(y, array[..., :width], array[..., width:])
        far = send(other, 2)
        passed = far if gate is None else after(far, gate, sink)
        return mine, far, send(mine, 1), send(passed, 1)

    columns = fast_second.reshape(2, own_rows, 2 * planes, 2, own_rows)
    split = [columns[:, :, :, i].reshape(2, own_rows, half) for i in range(2)]
    second_same, second_other = pick(c, split[0], split[1])
    same = jnp.concatenate([fast_first, fast_third, second_same], axis=2)
    same_mine, same_far = pick(y, same[0], same[1])
    near_mine, near_far = pick(y, second_other[0], second_other[1])
    same_far = send(same_far, 2)
    near_mine, near_far = send(near_mine, 1), send(near_far, 3)
    layers = ordered(y, same_mine[:, : 2 * width], same_far[:, : 2 * width], 0)
    second_mine = ordered(c, same_mine[:, 2 * width :], near_mine, 0)
    second_far = ordered(c, same_far[:, 2 * width :], near_far, 0)
    zero = jnp.concatenate([layers, ordered(y, second_mine, second_far, 1)], axis=1)
    names = ("steps0", "steps1", "out0", "new0", "new1", "out1", "out2")
    behind = {name: [] for name in names}
    full_zero = spread_on(spread(zero), behind["steps0"])

    scaled = learn_rates[:2, :, :, None] * value_tokens[:2].reshape(2, tokens, 2, width).astype(WIDE)
    scaled = scaled.astype(LOW).reshape(2, tokens, 2 * width)
    pairs = [jnp.stack([key_tokens[b], scaled[b]]) for b in range(2)]
    flat = (rows, 3 * width)
    unit = 2 * 4 * tokens * width * half
    where = lax.axis_index("plane").astype(jnp.int32).reshape(1)
    held = [((half, width), LOW), ((half, width), LOW), ((width, half), LOW)]

    def steps(block):
        kernel = functools.partial(steps_kernel, planes)
        outs = [(flat, WIDE if d % 2 == 0 else LOW) for d in range(planes)]
        made = [(s, WIDE) for s, _ in held]
        made = call(
            kernel,
            outs,
            6 * unit,
            where,
            *full_zero,
            *pairs[block],
            scratch=held + made,
            behind=behind["steps%d" % block],
        )
        return [[part] for part in made]

    def readout(block, full):
        kernel = functools.partial(readout_kernel, planes, block)
        outs = [((2 * tokens, width), WIDE), ((2 * tokens, width), LOW)]
        kept, sent = call(
            kernel,
            outs,
            3 * unit,
            where,
            *full,
            *queries,
            scratch=held,
            behind=behind["out%d" % block],
        )
        return (kept + send(sent, 1).astype(WIDE)).astype(LOW)

    def returned(total):
        return ordered(y, total[:tokens], send(total[tokens:], 2), 1)

    pairs[0] = to_quad(
        after(pairs[0], [zero], behind["new0"]),
        [full_zero[1], full_zero[planes // 2]],
        behind["steps0"],
    )
    zeros = steps(0)
    halve(zeros, 1, totals(zeros, 1), True)
    came = [zeros[d][-1] for d in range(2, planes, 2)]
    pairs[1] = to_quad(
        after(pairs[1], pairs[0], behind["steps1"]), came or zeros[0], behind["steps1"]
    )
    bit = 2
    while bit < planes:
        sent = totals(zeros, bit)
        behind["steps1"].extend(sent.values())
        halve(zeros, bit, sent, True)
        bit *= 2
    ones = steps(1)
    bit = 1
    while bit < planes:
        sent = totals(ones, bit)
        halve(ones, bit, sent, False)
        bit *= 2
    got_zero, got_one = zeros[0], ones[0]
    behind["new0"].extend(sent.values())

    sums_shape = (rows, 128)
    flat_sums = [(sums_shape, WIDE)]
    step_zero, moved, sums = call(
        first_moved_kernel,
        [(flat, WIDE), (flat, WIDE), ((2 * rows, 128), WIDE)],
        0,
        zero,
        *got_zero,
        behind=behind["new0"],
    )
    decay = jnp.broadcast_to(jnp.where(y == 0, momentum_decay[0], momentum_decay[1]), (8, 128))
    base, payload, old_sums = call(
        scaled_kernel,
        [(flat, WIDE), (flat, LOW)] + flat_sums,
        0,
        moved,
        step_zero,
        decay,
        got_one[0],
        sums,
        send(sums, 1),
    )
    half_way = planes // 2
    first_one = spread(payload)
    direct_one = to_plane(payload, 1)
    queries = to_quad(
        after(query_tokens, pairs[1], behind["out0"]), [old_sums], behind["out0"]
    )
    far_old = send(old_sums, 1)
    moved, sums = call(
        second_moved_kernel,
        [(flat, WIDE)] + flat_sums,
        0,
        base,
        *got_one[1:],
        behind=behind["new1"],
    )
    waited = (send(sums, 1), first_one[half_way], direct_one)
    far, first_one[half_way], direct_one = lax.optimization_barrier(waited)
    payload = call(last_scaled_kernel, [(flat, LOW)], 0, moved, sums, far, old_sums, far_old)[0]
    first_two = spread(payload)
    direct_two = to_plane(payload, 1)
    full_one = spread_on(first_one)
    full_one[1] = direct_one
    waited = (first_two[half_way], direct_two, queries[0], full_one[planes - 1])
    first_two[half_way], direct_two, first_query, full_one[planes - 1] = (
        lax.optimization_barrier(waited)
    )
    queries = (first_query,) + queries[1:]
    full_two = spread_on(first_two)
    full_two[1] = direct_two
    out_zero = returned(readout(0, full_zero))
    total_one = readout(1, full_one)
    waited = (full_two[planes - 1], out_zero, total_one)
    full_two[planes - 1], out_zero, total_one = lax.optimization_barrier(waited)
    out_one = returned(total_one)
    out_two = returned(readout(2, full_two))
    return jnp.stack([out_zero, out_one, out_two])


def solution(mesh):
    groups, count = mesh.shape["groups"], mesh.shape["tok"]
    split = Mesh(mesh.devices.reshape(groups, count // 4, 4), ("groups", "plane", "quad"))
    everywhere = P(None, ("groups", "plane", "quad"), None)
    rows = P(None, ("plane", "quad"), None)
    return jax.shard_map(
        shards,
        mesh=split,
        in_specs=(everywhere,) * 4 + (rows,) * 3 + (P(),),
        out_specs=everywhere,
        check_vma=False,
    )
```

```python
import functools

import jax
import jax.numpy as jnp
from jax import lax
from jax.experimental import pallas as pl
from jax.experimental.pallas import tpu as pltpu
from jax.sharding import Mesh, PartitionSpec as P

LOW = jnp.bfloat16
WIDE = jnp.float32


def call(kernel, outs, flops, *operands, scratch=(), behind=()):
    inner, used = kernel, len(operands)

    def kernel(*refs):
        inner(*refs[:used], *refs[used + len(behind) :])

    shapes = [jax.ShapeDtypeStruct(s, d) for s, d in outs]
    return pl.pallas_call(
        kernel,
        out_shape=shapes,
        in_specs=[
            pl.BlockSpec(memory_space=pltpu.SMEM if a.ndim == 1 else pltpu.VMEM) for a in operands
        ]
        + [pl.BlockSpec(memory_space=pl.ANY)] * len(behind),
        out_specs=[pl.BlockSpec(memory_space=pltpu.VMEM)] * len(shapes),
        scratch_shapes=[pltpu.VMEM(s, d) for s, d in scratch],
        compiler_params=pltpu.CompilerParams(vmem_limit_bytes=20 * 2**20),
        cost_estimate=pl.CostEstimate(flops=flops, bytes_accessed=1024, transcendentals=0),
    )(*operands, *behind)


def after(value, others, sink):
    value, others = lax.optimization_barrier((value, list(others)))
    sink.extend(others)
    return value


def dot(a, b, dims):
    return lax.dot_general(a, b, ((dims[:1], dims[1:]), ((), ())), preferred_element_type=WIDE)


def place(pieces, where, first, third, second):
    rows, columns = pieces[0].shape
    width = columns // 3
    half = width // 2
    for distance, piece in enumerate(pieces):
        z = where[0] ^ distance
        at = pl.multiple_of(z * rows, rows)
        first[pl.ds(at, rows), :] = piece[:, :width]
        third[pl.ds(at, rows), :] = piece[:, width : 2 * width]
        for y in range(2):
            start = 2 * width + y * half
            at = pl.multiple_of((2 * z + y) * rows, rows)
            second[pl.ds(at, rows), :] = piece[:, start : start + half]


def steps_kernel(planes, where, *refs):
    pieces, parts, refs = refs[:planes], refs[planes : planes + 4], refs[planes + 4 :]
    sent, (first, third, second, new_first, new_third, new_second) = refs[:planes], refs[planes:]
    rows, columns = pieces[0].shape
    width = columns // 3
    half = width // 2
    place(pieces, where, first, third, second)
    keys = jnp.concatenate([p[0] for p in parts], axis=0)
    scaled = jnp.concatenate([p[1] for p in parts], axis=0)
    pre_gate = dot(keys, first[...], (1, 1))
    pre_up = dot(keys, third[...], (1, 1))
    back = dot(scaled, second[...], (1, 0))
    sig_gate = jax.nn.sigmoid(pre_gate)
    silu = pre_gate * sig_gate
    hidden = (silu * pre_up).astype(LOW)
    d_gate = (back * pre_up * sig_gate * (1.0 + pre_gate * (1.0 - sig_gate))).astype(LOW)
    d_up = (back * silu).astype(LOW)
    new_first[...] = dot(d_gate, keys, (0, 0))
    new_third[...] = dot(d_up, keys, (0, 0))
    new_second[...] = dot(scaled, hidden, (0, 0))
    for distance, out in enumerate(sent):
        z = where[0] ^ distance
        at = pl.ds(pl.multiple_of(z * rows, rows), rows)
        out[:, :width] = new_first[at, :].astype(out.dtype)
        out[:, width : 2 * width] = new_third[at, :].astype(out.dtype)
        for y in range(2):
            start = 2 * width + y * half
            at = pl.ds(pl.multiple_of((2 * z + y) * rows, rows), rows)
            out[:, start : start + half] = new_second[at, :].astype(out.dtype)


def readout_kernel(planes, block, where, *refs):
    pieces, parts, refs = refs[:planes], refs[planes : planes + 4], refs[planes + 4 :]
    kept, sent, first, third, second = refs
    tokens = kept.shape[0] // 2
    place(pieces, where, first, third, second)
    inputs = jnp.concatenate([p[block] for p in parts], axis=0)
    pre_gate = dot(inputs, first[...], (1, 1))
    pre_up = dot(inputs, third[...], (1, 1))
    hidden = (pre_gate * jax.nn.sigmoid(pre_gate) * pre_up).astype(LOW)
    result = dot(hidden, second[...], (1, 1))
    kept[...] = result[: 2 * tokens]
    sent[...] = result[2 * tokens :].astype(LOW)


def square_sums(array, width):
    half = width // 2
    columns = []
    for y in range(2):
        piece = array[:, 2 * width + y * half : 2 * width + (y + 1) * half]
        columns.append(jnp.sum(piece * piece, axis=1, keepdims=True))
    return columns


def sums_of(array, width):
    parts = [array[:, m * width : (m + 1) * width] for m in range(2)]
    parts = [jnp.sum(p * p, axis=1, keepdims=True) for p in parts] + square_sums(array, width)
    return jnp.concatenate(parts + [jnp.zeros((array.shape[0], 124), WIDE)], axis=1)


def first_moved_kernel(old, *refs):
    got, (momentum, moved, sums) = refs[:-3], refs[-3:]
    rows, width = old.shape[0], old.shape[1] // 3
    total = got[0][...].astype(WIDE)
    for part in got[1:]:
        total = total + part[...].astype(WIDE)
    before = old[...].astype(WIDE)
    after_step = before + total
    momentum[...] = total
    moved[...] = after_step
    sums[:rows, :] = sums_of(after_step, width)
    sums[rows:, :] = sums_of(before, width)


def second_moved_kernel(base, *refs):
    got, (moved, sums) = refs[:-2], refs[-2:]
    total = base[...]
    for part in got:
        total = total + part[...].astype(WIDE)
    moved[...] = total
    sums[...] = sums_of(total, total.shape[1] // 3)


def factors(sums, far_sums, old_sums, far_old_sums):
    def whole(mine, far, m):
        return mine[:, m : m + 1] + (far[:, m : m + 1] if m > 1 else 0.0)

    return [
        jnp.sqrt(whole(old_sums, far_old_sums, m) + 1e-06)
        / jnp.sqrt(whole(sums, far_sums, m) + 1e-06)
        for m in range(4)
    ]


def rescaled(moved, scales):
    width = moved.shape[1] // 3
    half = width // 2
    edges = [0, width, 2 * width, 2 * width + half, 3 * width]
    pieces = [moved[:, edges[m] : edges[m + 1]] * scales[m] for m in range(4)]
    return jnp.concatenate(pieces, axis=1)


def scaled_kernel(moved, momentum, decay, part, sums, far, base, payload, new_sums):
    rows = moved.shape[0]
    new, old = slice(0, rows), slice(rows, None)
    result = rescaled(moved, factors(sums[new], far[new], sums[old], far[old]))
    payload[...] = result.astype(LOW)
    new_sums[...] = sums_of(result, result.shape[1] // 3)
    base[...] = result + (decay[0:1, 0:1] * momentum[...] + part[...])


def last_scaled_kernel(moved, sums, far, old, far_old, payload):
    payload[...] = rescaled(moved, factors(sums, far, old, far_old)).astype(LOW)


def shards(
    query_tokens,
    key_tokens,
    value_tokens,
    learn_rates,
    fast_first,
    fast_third,
    fast_second,
    momentum_decay,
):
    planes = lax.axis_size("plane")
    index = lax.axis_index("quad")
    y, c = index // 2, index % 2
    width = fast_first.shape[2]
    half = width // 2
    own_rows = fast_first.shape[1]
    rows = 2 * own_rows
    tokens = key_tokens.shape[1]

    def send(array, offset):
        return lax.ppermute(array, "quad", [(q, q ^ offset) for q in range(4)])

    def to_plane(array, bit):
        return lax.ppermute(array, "plane", [(z, z ^ bit) for z in range(planes)])

    def spread(own):
        return {0: own, planes // 2: to_plane(own, planes // 2)}

    def spread_on(pieces, sink=None):
        bit = planes // 4
        while bit:
            direct = to_plane(pieces[0], bit)
            for distance in list(pieces):
                if distance:
                    piece = pieces[distance]
                    if sink is not None:
                        piece = after(piece, [direct], sink)
                    pieces[distance | bit] = to_plane(piece, bit)
            pieces[bit] = direct
            bit //= 2
        return [pieces[d] for d in range(planes)]

    def totals(parts, bit):
        return {
            d: sum(p.astype(WIDE) for p in parts[d]).astype(LOW)
            for d in range(planes - bit, 0, -2 * bit)
        }

    def halve(parts, bit, sent, relayed_first):
        relayed = None
        for distance, total in sent.items():
            if relayed_first and distance == bit and relayed is not None:
                total, came = lax.optimization_barrier((total, parts[relayed][-1]))
                parts[relayed][-1] = came
            parts[distance ^ bit].append(to_plane(total, bit))
            relayed = distance ^ bit

    def pick(flag, a, b):
        return jnp.where(flag == 0, a, b), jnp.where(flag == 0, b, a)

    def ordered(flag, a, b, axis):
        return jnp.where(flag == 0, jnp.concatenate([a, b], axis), jnp.concatenate([b, a], axis))

    def to_quad(array, gate=None, sink=None):
        mine, other = pick(y, array[..., :width], array[..., width:])
        far = send(other, 2)
        passed = far if gate is None else after(far, gate, sink)
        return mine, far, send(mine, 1), send(passed, 1)

    columns = fast_second.reshape(2, own_rows, 2 * planes, 2, own_rows)
    split = [columns[:, :, :, i].reshape(2, own_rows, half) for i in range(2)]
    second_same, second_other = pick(c, split[0], split[1])
    same = jnp.concatenate([fast_first, fast_third, second_same], axis=2)
    same_mine, same_far = pick(y, same[0], same[1])
    near_mine, near_far = pick(y, second_other[0], second_other[1])
    same_far = send(same_far, 2)
    near_mine, near_far = send(near_mine, 1), send(near_far, 3)
    layers = ordered(y, same_mine[:, : 2 * width], same_far[:, : 2 * width], 0)
    second_mine = ordered(c, same_mine[:, 2 * width :], near_mine, 0)
    second_far = ordered(c, same_far[:, 2 * width :], near_far, 0)
    zero = jnp.concatenate([layers, ordered(y, second_mine, second_far, 1)], axis=1)
    names = ("steps0", "steps1", "out0", "new0", "new1", "out1", "out2")
    behind = {name: [] for name in names}
    full_zero = spread_on(spread(zero), behind["steps0"])

    scaled = learn_rates[:2, :, :, None] * value_tokens[:2].reshape(2, tokens, 2, width).astype(WIDE)
    scaled = scaled.astype(LOW).reshape(2, tokens, 2 * width)
    pairs = [jnp.stack([key_tokens[b], scaled[b]]) for b in range(2)]
    flat = (rows, 3 * width)
    unit = 2 * 4 * tokens * width * half
    where = lax.axis_index("plane").astype(jnp.int32).reshape(1)
    held = [((half, width), LOW), ((half, width), LOW), ((width, half), LOW)]

    def steps(block):
        kernel = functools.partial(steps_kernel, planes)
        outs = [(flat, WIDE if d % 2 == 0 else LOW) for d in range(planes)]
        made = [(s, WIDE) for s, _ in held]
        made = call(
            kernel,
            outs,
            6 * unit,
            where,
            *full_zero,
            *pairs[block],
            scratch=held + made,
            behind=behind["steps%d" % block],
        )
        return [[part] for part in made]

    def readout(block, full):
        kernel = functools.partial(readout_kernel, planes, block)
        outs = [((2 * tokens, width), WIDE), ((2 * tokens, width), LOW)]
        kept, sent = call(
            kernel,
            outs,
            3 * unit,
            where,
            *full,
            *queries,
            scratch=held,
            behind=behind["out%d" % block],
        )
        return (kept + send(sent, 1).astype(WIDE)).astype(LOW)

    def returned(total):
        return ordered(y, total[:tokens], send(total[tokens:], 2), 1)

    pairs[0] = to_quad(
        after(pairs[0], [zero], behind["new0"]),
        [full_zero[1], full_zero[planes // 2]],
        behind["steps0"],
    )
    zeros = steps(0)
    halve(zeros, 1, totals(zeros, 1), True)
    came = [zeros[d][-1] for d in range(2, planes, 2)]
    pairs[1] = to_quad(
        after(pairs[1], pairs[0], behind["steps1"]), came or zeros[0], behind["steps1"]
    )
    bit = 2
    while bit < planes:
        sent = totals(zeros, bit)
        behind["steps1"].extend(sent.values())
        halve(zeros, bit, sent, True)
        bit *= 2
    ones = steps(1)
    bit = 1
    while bit < planes:
        sent = totals(ones, bit)
        halve(ones, bit, sent, False)
        bit *= 2
    got_zero, got_one = zeros[0], ones[0]
    behind["new0"].extend(sent.values())

    sums_shape = (rows, 128)
    flat_sums = [(sums_shape, WIDE)]
    step_zero, moved, sums = call(
        first_moved_kernel,
        [(flat, WIDE), (flat, WIDE), ((2 * rows, 128), WIDE)],
        0,
        zero,
        *got_zero,
        behind=behind["new0"],
    )
    decay = jnp.broadcast_to(jnp.where(y == 0, momentum_decay[0], momentum_decay[1]), (8, 128))
    base, payload, old_sums = call(
        scaled_kernel,
        [(flat, WIDE), (flat, LOW)] + flat_sums,
        0,
        moved,
        step_zero,
        decay,
        got_one[0],
        sums,
        send(sums, 1),
    )
    half_way = planes // 2
    first_one = spread(payload)
    direct_one = to_plane(payload, 1)
    queries = to_quad(
        after(query_tokens, pairs[1], behind["out0"]), [old_sums], behind["out0"]
    )
    far_old = send(old_sums, 1)
    moved, sums = call(
        second_moved_kernel,
        [(flat, WIDE)] + flat_sums,
        0,
        base,
        *got_one[1:],
        behind=behind["new1"],
    )
    waited = (send(sums, 1), first_one[half_way], direct_one)
    far, first_one[half_way], direct_one = lax.optimization_barrier(waited)
    payload = call(last_scaled_kernel, [(flat, LOW)], 0, moved, sums, far, old_sums, far_old)[0]
    first_two = spread(payload)
    direct_two = to_plane(payload, 1)
    full_one = spread_on(first_one)
    full_one[1] = direct_one
    waited = (first_two[half_way], direct_two, queries[0], full_one[planes - 1])
    first_two[half_way], direct_two, first_query, full_one[planes - 1] = (
        lax.optimization_barrier(waited)
    )
    queries = (first_query,) + queries[1:]
    full_two = spread_on(first_two)
    full_two[1] = direct_two
    total_zero = readout(0, full_zero)
    total_one = readout(1, full_one)
    both = jnp.stack([total_zero, total_one])
    far_both = send(both[:, tokens:], 2)
    full_two[planes - 1], far_both = lax.optimization_barrier((full_two[planes - 1], far_both))
    out_zero = ordered(y, both[0, :tokens], far_both[0], 1)
    out_one = ordered(y, both[1, :tokens], far_both[1], 1)
    out_two = returned(readout(2, full_two))
    return jnp.stack([out_zero, out_one, out_two])


def solution(mesh):
    groups, count = mesh.shape["groups"], mesh.shape["tok"]
    split = Mesh(mesh.devices.reshape(groups, count // 4, 4), ("groups", "plane", "quad"))
    everywhere = P(None, ("groups", "plane", "quad"), None)
    rows = P(None, ("plane", "quad"), None)
    return jax.shard_map(
        shards,
        mesh=split,
        in_specs=(everywhere,) * 4 + (rows,) * 3 + (P(),),
        out_specs=everywhere,
        check_vma=False,
    )
```
